32 devices in a mesh: rows: 8 (over y, x, core), cols: 4 (over z).
Axes of the slice: x: 2, y: 2, z: 4, core: 2. Of those that a mesh axis runs over, the one named last changes fastest.
Arguments:
- krylov: bfloat16 [8192, 256], P(('rows', 'cols')), may hold values from -6 to 6
- geometry: float32 [7, 8192], P(None, ('rows', 'cols')), may hold values from -1 to 2, as said below
- corr_index: int32 [8, 8192], P(None, ('rows', 'cols')), may hold values from 0 to 8191, as said below
- corr_weight: float32 [16, 8192], P(None, ('rows', 'cols')), may hold values from -1.5 to 1.5
- blades: int32 [128], replicated, may hold values from 3 to 8
- harmonic: int32 [128], replicated, may hold values from 1 to 4
- observer_angles: float32 [2, 2048], replicated, may hold values from -3.140625 to 3.140625
Outputs:
- residual: float32 [8192, 256], P(('rows', 'cols'))
- far_field: float32 [2048, 256], P(('rows', 'cols'))
The draws below stay inside these ranges and needn't reach their ends.
Inputs may be any that keep to these rules, and one draw needn't show every extreme that they name: `geometry`: centers lie on a duct of radius about 1 with heights 0 to 2 and on a centerbody of radius 0.35; normals have unit length; areas are positive. corr_index[c, i] lies in the same aligned block of 256 consecutive panels as panel i.
All inputs are finite; a program needn't handle non-finite values.
Results may differ from the reference program's by a relative error of at most 0.0029.
Values may be sent and summed in bfloat16 or wider, within the bound.
No kernel may reach another device: no remote copies, remote signals or barrier semaphores. Data moves between devices by JAX's collectives and lax.ppermute only.
A program may use at most 64 MiB of HBM per device.

```python
import math
import jax
import jax.numpy as jnp
from jax import lax

PANELS_DEV = 256
NV = 128
NC = 8
NS = 64
NP = 8192
NOBS = 2048


def draw_geometry(key, part):
    keys = jax.random.split(jax.random.fold_in(key, 11), 5)
    choose = jax.random.uniform(keys[0], (NP,), jnp.float32)
    theta = jax.random.uniform(keys[1], (NP,), jnp.float32, 0.0, 2.0 * math.pi)
    height = jax.random.uniform(keys[2], (NP,), jnp.float32)
    slope = jax.random.uniform(keys[3], (NP,), jnp.float32, -0.2, 0.2)
    duct = choose < 0.7
    radius = jnp.where(duct, 1.0, 0.35)
    pos_z = jnp.where(duct, 2.0 * height, 0.3 + 1.4 * height)
    sign = jnp.where(duct, -1.0, 1.0)
    scale = 1.0 / jnp.sqrt(1.0 + slope * slope)
    spread = jax.random.uniform(keys[4], (NP,), jnp.float32, math.log(0.5), math.log(2.0))
    area = 16.0 / NP * jnp.exp(spread)
    return jnp.stack([radius * jnp.cos(theta), radius * jnp.sin(theta), pos_z, sign * jnp.cos(theta) * scale, sign * jnp.sin(theta) * scale, slope * scale, area]).astype(jnp.float32)


def draw_corr_index(key, part):
    offsets = jax.random.randint(jax.random.fold_in(key, 23), (NC, NP), 0, PANELS_DEV, dtype=jnp.int32)
    base = jnp.arange(NP, dtype=jnp.int32) // PANELS_DEV * PANELS_DEV
    return (base[None, :] + offsets).astype(jnp.int32)


def set_ends(values, key, least, largest):
    shape = values.shape
    place = [jax.random.randint(jax.random.fold_in(key, axis), (), 0, shape[axis]) for axis in range(len(shape))]
    values = values.at[tuple(place)].set(least)
    longest = shape.index(max(shape))
    place[longest] = (place[longest] + 1) % shape[longest]
    return values.at[tuple(place)].set(largest)


def level_of(stream_key, dims, cuts, least, high):
    def one(axis_at, shards_of):
        draws = jax.random.uniform(jax.random.fold_in(jax.random.fold_in(stream_key, 6), axis_at), (shards_of,), jnp.float32, least / len(cuts), high / len(cuts))
        return jnp.repeat(jnp.exp(draws), dims[axis_at] // shards_of).reshape((-1,) + (1,) * (len(dims) - axis_at - 1))

    factor_of = one(*cuts[0])
    for cut in cuts[1:]:
        factor_of = factor_of * one(*cut)
    return factor_of


def noise(rng, shape, scale, reach, pieces=(), held_as=jnp.bfloat16):
    array = scale * jax.random.normal(rng, shape, jnp.float32)
    if pieces:
        array = array * level_of(rng, shape, pieces, -0.22, 0.18)
    return jnp.clip(array, -reach, reach).astype(held_as)


def setup_inputs(seed: int = 0) -> dict:
    seeds = jax.random.split(jax.random.key(seed), 8)
    krylov = noise(seeds[0], (NP, 2 * NV), 1.0, 6.0, ((0, 32),))
    geometry = draw_geometry(jax.random.fold_in(seeds[7], 71), 0)
    corr_index = draw_corr_index(jax.random.fold_in(seeds[7], 71), 0)
    corr_weight = noise(seeds[3], (2 * NC, NP), 0.3, 1.5, ((1, 32),), jnp.float32)
    blades = set_ends(jax.random.randint(seeds[4], (NV,), 3, 9), jax.random.fold_in(seeds[4], 1), 3, 8).astype(jnp.int32)
    harmonic = set_ends(jax.random.randint(seeds[5], (NV,), 1, 5), jax.random.fold_in(seeds[5], 1), 1, 4).astype(jnp.int32)
    observer_angles = jnp.clip(jax.random.uniform(seeds[6], (2, NOBS), jnp.float32, -3.140625, 3.140625), -3.140625, 3.140625)
    return {"krylov": krylov, "geometry": geometry, "corr_index": corr_index, "corr_weight": corr_weight, "blades": blades, "harmonic": harmonic, "observer_angles": observer_angles}


wavenumber = 20.0
cycle_radius = 0.7
cycle_height = 1.0
four_pi = 4.0 * math.pi

def green_parts(r_sq):
    inverse = lax.rsqrt(r_sq)
    phase = wavenumber * r_sq * inverse
    g_re = jnp.cos(phase) * inverse / four_pi
    g_im = jnp.sin(phase) * inverse / four_pi
    f_re = (-g_re * inverse - wavenumber * g_im) * inverse
    f_im = (-g_im * inverse + wavenumber * g_re) * inverse
    return (g_re, g_im, f_re, f_im)

def panel_tile(row_geom, col_geom, row_ids, col_ids, soft_sq):
    dx = row_geom[0][:, None] - col_geom[0][None, :]
    dy = row_geom[1][:, None] - col_geom[1][None, :]
    dz = row_geom[2][:, None] - col_geom[2][None, :]
    r_sq = dx * dx + dy * dy + dz * dz + soft_sq
    g_re, g_im, f_re, f_im = green_parts(r_sq)
    along_col = -(dx * col_geom[3][None, :] + dy * col_geom[4][None, :] + dz * col_geom[5][None, :])
    along_row = (dx * row_geom[3][:, None] + dy * row_geom[4][:, None] + dz * row_geom[5][:, None]) / wavenumber
    area = col_geom[6][None, :]
    t_re = area * (f_re * along_col - f_im * along_row)
    t_im = area * (f_re * along_row + f_im * along_col)
    same = row_ids[:, None] == col_ids[None, :]
    zeros = jnp.zeros_like(t_re)
    return (jnp.where(same, zeros, t_re).astype(jnp.bfloat16), jnp.where(same, zeros, t_im).astype(jnp.bfloat16))

def apply_tile(t_re, t_im, vectors):
    nvec = vectors.shape[1] // 2
    first = jnp.dot(t_re, vectors, preferred_element_type=jnp.float32)
    second = jnp.dot(t_im, vectors, preferred_element_type=jnp.float32)
    return jnp.concatenate([first[:, :nvec] - second[:, nvec:], first[:, nvec:] + second[:, :nvec]], axis=1)

def far_tile(angles, geom):
    sin_t = jnp.sin(angles[0])
    dir_x = sin_t * jnp.cos(angles[1])
    dir_y = sin_t * jnp.sin(angles[1])
    dir_z = jnp.cos(angles[0])
    along = dir_x[:, None] * geom[0][None, :] + dir_y[:, None] * geom[1][None, :] + dir_z[:, None] * geom[2][None, :]
    normal_part = dir_x[:, None] * geom[3][None, :] + dir_y[:, None] * geom[4][None, :] + dir_z[:, None] * geom[5][None, :]
    phase = -wavenumber * along
    scale = geom[6][None, :] * wavenumber * normal_part
    t_re = scale * jnp.sin(phase)
    t_im = -scale * jnp.cos(phase)
    return (t_re.astype(jnp.bfloat16), t_im.astype(jnp.bfloat16))

def incident(geom, blades, harmonic):
    angle = 2.0 * math.pi * jnp.arange(NS, dtype=jnp.float32) / NS
    src_x = cycle_radius * jnp.cos(angle)
    src_y = cycle_radius * jnp.sin(angle)
    dx = geom[0][:, None] - src_x[None, :]
    dy = geom[1][:, None] - src_y[None, :]
    dz = geom[2][:, None] - cycle_height
    r_sq = dx * dx + dy * dy + dz * dz
    g_re, g_im, f_re, f_im = green_parts(r_sq)
    normal_part = (dx * geom[3][:, None] + dy * geom[4][:, None] + dz * geom[5][:, None]) / wavenumber
    h_re = g_re - f_im * normal_part
    h_im = g_im + f_re * normal_part
    modes = (blades * harmonic).astype(jnp.float32)
    e_re = jnp.cos(angle[:, None] * modes[None, :])
    e_im = jnp.sin(angle[:, None] * modes[None, :])
    high = lax.Precision.HIGHEST
    b_re = jnp.dot(h_re, e_re, precision=high) - jnp.dot(h_im, e_im, precision=high)
    b_im = jnp.dot(h_re, e_im, precision=high) + jnp.dot(h_im, e_re, precision=high)
    return jnp.concatenate([b_re, b_im], axis=1)

def correction(values, index_local, weights):
    count = index_local.shape[0]
    nvec = values.shape[1] // 2
    nearby = values[index_local]
    w_re = weights[:count][:, :, None]
    w_im = weights[count:][:, :, None]
    part_re = lax.optimization_barrier(jnp.sum(w_re * nearby[:, :, :nvec] - w_im * nearby[:, :, nvec:], axis=0))
    part_im = lax.optimization_barrier(jnp.sum(w_re * nearby[:, :, nvec:] + w_im * nearby[:, :, :nvec], axis=0))
    return jnp.concatenate([part_re, part_im], axis=1)

def reference(krylov, geometry, corr_index, corr_weight, blades, harmonic, observer_angles):
    soft_sq = 4.0 / NP
    panel_ids = jnp.arange(NP, dtype=jnp.int32)
    row_block = math.gcd(NP, 512)

    def one_block(step):
        start = (step * row_block).astype(jnp.int32)
        geom = lax.dynamic_slice_in_dim(geometry, start, row_block, 1)
        ids = lax.dynamic_slice_in_dim(panel_ids, start, row_block, 0)
        t_re, t_im = panel_tile(geom, geometry, ids, panel_ids, soft_sq)
        return apply_tile(t_re, t_im, krylov)
    applied = lax.map(one_block, jnp.arange(NP // row_block, dtype=jnp.int32)).reshape(NP, 2 * NV)
    values = krylov.astype(jnp.float32)
    near = correction(values, corr_index, corr_weight)
    source = incident(geometry, blades, harmonic)
    residual = source - (0.5 * values + near + applied)
    obs_block = math.gcd(NOBS, 512)

    def one_far(step):
        start = (step * obs_block).astype(jnp.int32)
        angles = lax.dynamic_slice_in_dim(observer_angles, start, obs_block, 1)
        t_re, t_im = far_tile(angles, geometry)
        return apply_tile(t_re, t_im, krylov)
    far_field = lax.map(one_far, jnp.arange(NOBS // obs_block, dtype=jnp.int32)).reshape(NOBS, 2 * NV)
    return (residual, far_field)
```

```python
import functools
import math

import jax
import jax.numpy as jnp
from jax import lax
from jax.experimental import pallas as pl
from jax.experimental.pallas import tpu as pltpu
from jax.sharding import PartitionSpec as P

NS = 64
wavenumber = 20.0
cycle_radius = 0.7
cycle_height = 1.0
four_pi = 4.0 * math.pi
two_pi = 2.0 * math.pi

COARSE_D = (-4.203673078505327, 0.9884209687656514)
COARSE_N = (-2.9883226762430346, 3.1051740325541175)
FINE_D = (-2.7704097493600783, 0.6301024476540067)
FINE_N = (0.21837236917008357, -2.1911377274692434, 1.9795254225510943)
ROUNDER = 12582912.0

turns_sq = (wavenumber / two_pi) ** 2
tile_scale = wavenumber**3 / four_pi / two_pi**2
DEPTH = 48
CHUNK = 256
SUB = 16
BF16 = jnp.bfloat16
F32 = jnp.float32


def half_tangent(turn, fine=False):
    f = turn - ((turn + ROUNDER) - ROUNDER)
    z = f * f
    if fine:
        d = (z + FINE_D[0]) * z + FINE_D[1]
        x = f * ((z * FINE_N[0] + FINE_N[1]) * z + FINE_N[2])
    else:
        d = (z + COARSE_D[0]) * z + COARSE_D[1]
        x = f * (z * COARSE_N[0] + COARSE_N[1])
    return d, x


def cos_sin(turn):
    d, x = half_tangent(turn, fine=True)
    q = 1.0 / (d * d + x * x)
    return (d * d - x * x) * q, 2.0 * d * x * q


def parts(v):
    high = v.astype(BF16).astype(F32)
    rest = v - high
    mid = rest.astype(BF16).astype(F32)
    return high, mid, rest - mid


def column_features(geom_refs, out_s, out_u, out_w, vec):
    at = 0
    for ref in geom_refs:
        g = ref[...]
        piece = g.shape[1]
        where = pl.ds(at, piece)
        x, y, z = g[0:1], g[1:2], g[2:3] - 1.0
        area = g[6:7] * tile_scale
        zero = jnp.zeros((4, piece), F32)
        dot_cn = x * g[3:4] + y * g[4:5] + z * g[5:6]
        vec[0:1], vec[1:2], vec[2:3] = x, y, z
        vec[3:4] = jnp.ones((1, piece), F32)
        vec[4:8] = zero
        vec[4:5] = turns_sq * (x * x + y * y + z * z)
        put_columns(out_s, where, vec[...])
        vec[0:3] = -area * g[3:6]
        vec[3:4] = area * dot_cn
        vec[4:8] = zero
        put_columns(out_u, where, vec[...])
        vec[0:1], vec[1:2], vec[2:3] = area * x, area * y, area * z
        vec[3:4] = area
        put_columns(out_w, where, vec[...])
        at += piece


def put_columns(out, where, v):
    high, mid, low = parts(v)
    out[0:16, where] = jnp.concatenate([high, mid], axis=0).astype(BF16)
    out[16:32, where] = jnp.concatenate([high, low], axis=0).astype(BF16)
    out[32:48, where] = jnp.concatenate([high, mid], axis=0).astype(BF16)


def columns_kernel(count, *refs):
    column_features(refs[:count], *refs[count:])


def row_part(v):
    high, mid, low = parts(v)
    stacked = jnp.concatenate([high, high, mid, high, low, mid], axis=0)
    return stacked.T.astype(BF16)


def row_features(g, dirs, soft_sq, out_s, out_u, out_w, vec, small):
    piece = g.shape[1]
    each = dirs.shape[1]
    x, y, z = g[0:1], g[1:2], g[2:3] - 1.0
    zero = jnp.zeros((4, piece), F32)
    vec[4:8] = zero
    vec[0:1], vec[1:2], vec[2:3] = (-2.0 * turns_sq) * x, (-2.0 * turns_sq) * y, (-2.0 * turns_sq) * z
    vec[3:4] = turns_sq * (x * x + y * y + z * z + soft_sq)
    vec[4:5] = jnp.ones((1, piece), F32)
    out_s[0:piece] = row_part(vec[...])
    vec[0:1], vec[1:2], vec[2:3] = x, y, z
    vec[3:4] = jnp.ones((1, piece), F32)
    vec[4:8] = zero
    out_u[0:piece] = row_part(vec[...])
    vec[0:3] = g[3:6] * (-1.0 / wavenumber)
    vec[3:4] = (x * g[3:4] + y * g[4:5] + z * g[5:6]) * (1.0 / wavenumber)
    out_w[...] = row_part(vec[...])
    small[4:8] = jnp.zeros((4, each), F32)
    small[0:3] = dirs[0:3] * (-wavenumber / two_pi)
    small[3:4] = dirs[2:3] * (-wavenumber / two_pi)
    out_s[piece:] = row_part(small[...])
    small[0:3] = dirs[0:3] * (-wavenumber / tile_scale)
    small[3:4] = jnp.zeros((1, each), F32)
    out_u[piece:] = row_part(small[...])


def panel_entries(s, u, w):
    inverse = lax.rsqrt(s)
    d, x = half_tangent(s * inverse)
    d2, x2 = d * d, x * x
    q = pl.reciprocal((d2 + x2) * s)
    re = (d2 - x2) * q
    h = d * q
    im = (h + h) * x
    p = inverse * (1.0 / two_pi)
    a = p * u + w
    b = u - p * w
    return -(re * a + im * b), re * b - im * a


def far_entries(turn, scale):
    d, x = half_tangent(turn)
    d2, x2 = d * d, x * x
    q = scale * pl.reciprocal(d2 + x2)
    h = d * q
    return (h + h) * x, (x2 - d2) * q


def tiles_kernel(masked, soft_sq, g_ref, dirs_ref, cs, cu, cw, t_re, t_im, rs, ru, rw, vec, small, *bufs):
    piece = g_ref.shape[1]
    rows = t_re.shape[0]
    total = t_re.shape[1]
    row_features(g_ref[...], dirs_ref[...], soft_sq, rs, ru, rw, vec, small)

    def multiply(at, buf):
        where = pl.ds(pl.multiple_of(at * CHUNK, CHUNK), CHUNK)
        for row_ref, col_ref, out in ((rs, cs, buf[0]), (ru, cu, buf[1]), (rw, cw, buf[2])):
            out[...] = jnp.dot(row_ref[...], col_ref[:, where], preferred_element_type=F32)

    def entries(at, buf):
        where = pl.ds(pl.multiple_of(at * CHUNK, CHUNK), CHUNK)
        for begin in range(0, rows, SUB):
            take = pl.ds(begin, SUB)
            if begin < piece:
                re, im = panel_entries(buf[0][take], buf[1][take], buf[2][take])
            else:
                re, im = far_entries(buf[0][take], buf[1][take])
            t_re[take, where] = re.astype(BF16)
            t_im[take, where] = im.astype(BF16)

    first, second = bufs[:3], bufs[3:]
    multiply(0, first)

    def two(step, carry):
        multiply(2 * step + 1, second)
        entries(2 * step, first)
        multiply(jnp.minimum(2 * step + 2, total // CHUNK - 1), first)
        entries(2 * step + 1, second)
        return carry

    lax.fori_loop(0, total // (2 * CHUNK), two, 0)
    if masked:
        for begin in range(0, piece, CHUNK):
            corner = (pl.ds(begin, CHUNK), pl.ds(begin, CHUNK))
            down = lax.broadcasted_iota(jnp.int32, (CHUNK, CHUNK), 0)
            across = lax.broadcasted_iota(jnp.int32, (CHUNK, CHUNK), 1)
            for t in (t_re, t_im):
                held = t[corner].astype(F32)
                t[corner] = jnp.where(down == across, 0.0, held).astype(BF16)


def apply_kernel(count, out_dtype, t_re, t_im, *refs):
    vectors, out = refs[:count], refs[count]
    piece, width = vectors[0].shape
    half = width // 2
    first = jnp.zeros(out.shape, F32)
    second = jnp.zeros(out.shape, F32)
    for at, ref in enumerate(vectors):
        where = pl.ds(at * piece, piece)
        first += jnp.dot(t_re[:, where], ref[...], preferred_element_type=F32)
        second += jnp.dot(t_im[:, where], ref[...], preferred_element_type=F32)
    out[:, :half] = (first[:, :half] - second[:, half:]).astype(out_dtype)
    out[:, half:] = (first[:, half:] + second[:, :half]).astype(out_dtype)


def dot_first(left, right, precision=None):
    return lax.dot_general(
        left, right, (((0,), (0,)), ((), ())), precision=precision, preferred_element_type=F32
    )


def local_kernel(x_ref, g_ref, index_ref, weight_ref, mode_ref, out):
    piece, width = x_ref.shape
    half = width // 2
    count = index_ref.shape[0]
    rows = lax.axis_index("rows")
    cols = lax.axis_index("cols")
    base = (rows * lax.axis_size("cols") + cols) * piece
    ids = lax.broadcasted_iota(jnp.int32, (piece, piece), 0) + base
    m_re = jnp.zeros((piece, piece), F32)
    m_im = jnp.zeros((piece, piece), F32)
    for c in range(count):
        hit = ids == index_ref[c : c + 1]
        m_re += jnp.where(hit, weight_ref[c : c + 1], 0.0)
        m_im += jnp.where(hit, weight_ref[count + c : count + c + 1], 0.0)
    x = x_ref[...]
    first = jnp.zeros((piece, width), F32)
    second = jnp.zeros((piece, width), F32)
    for part in parts(m_re):
        first += dot_first(part.astype(BF16), x)
    for part in parts(m_im):
        second += dot_first(part.astype(BF16), x)
    g = g_ref[...]
    source = lax.broadcasted_iota(jnp.int32, (NS, 1), 0)
    src_cos, src_sin = cos_sin(source.astype(F32) * (1.0 / NS))
    dx = g[0:1] - cycle_radius * src_cos
    dy = g[1:2] - cycle_radius * src_sin
    dz = g[2:3] - cycle_height
    r_sq = dx * dx + dy * dy + dz * dz
    inverse = lax.rsqrt(r_sq)
    c, s = cos_sin(r_sq * inverse * (wavenumber / two_pi))
    g_re = c * inverse * (1.0 / four_pi)
    g_im = s * inverse * (1.0 / four_pi)
    slope = (dx * g[3:4] + dy * g[4:5] + dz * g[5:6]) * inverse
    f_re = 1.0 - slope
    f_im = slope * inverse * (-1.0 / wavenumber)
    h_re = g_re * f_re - g_im * f_im
    h_im = g_re * f_im + g_im * f_re
    turn = lax.rem(source * mode_ref[...], NS).astype(F32) * (1.0 / NS)
    e_re, e_im = cos_sin(turn)
    lhs = jnp.concatenate([h_re, h_im], axis=0)
    rhs = jnp.concatenate(
        [jnp.concatenate([e_re, e_im], axis=1), jnp.concatenate([-e_im, e_re], axis=1)], axis=0
    )
    b = dot_first(lhs, rhs, lax.Precision.HIGHEST)
    xf = x.astype(F32)
    out[:, :half] = b[:, :half] - 0.5 * xf[:, :half] - (first[:, :half] - second[:, half:])
    out[:, half:] = b[:, half:] - 0.5 * xf[:, half:] - (first[:, half:] + second[:, :half])


def final_kernel(count, base, own, *refs):
    got, residual, far = refs[:count], refs[count], refs[count + 1]
    piece = residual.shape[0]
    total = own[...]
    for ref in got:
        total += ref[...].astype(F32)
    residual[...] = base[...] - total[:piece]
    far[...] = total[piece:]


def call(kernel, out_shape, scratch=(), name=None, cost=None):
    return pl.pallas_call(
        kernel,
        out_shape=out_shape,
        scratch_shapes=list(scratch),
        compiler_params=pltpu.CompilerParams(vmem_limit_bytes=40 * 2**20),
        cost_estimate=cost,
        name=name,
    )


def xor_permute(value, axis, mask):
    size = lax.axis_size(axis)
    return lax.ppermute(value, axis, [(i, i ^ mask) for i in range(size)])


def local(krylov, geometry, corr_index, corr_weight, blades, harmonic, observer_angles):
    nrows = lax.axis_size("rows")
    ncols = lax.axis_size("cols")
    row_at = lax.axis_index("rows")
    col_at = lax.axis_index("cols")
    piece, width = krylov.shape
    panels = piece * nrows * ncols
    soft_sq = 4.0 / panels
    each = observer_angles.shape[1] // (nrows * ncols)
    rows = piece + each

    line_masks = list(range(1, ncols))
    plane_masks = list(range(2, nrows, 2))
    geom_line = [geometry] + [xor_permute(geometry, "cols", m) for m in line_masks]
    geom_plane = [geometry] + [xor_permute(geometry, "rows", m) for m in plane_masks]
    geom_other = [xor_permute(g, "rows", 1) for g in geom_line]
    x_line = [krylov] + [xor_permute(krylov, "cols", m) for m in line_masks]
    x_other = [xor_permute(x, "rows", 1) for x in x_line]
    sources = geom_line + geom_other
    vectors = x_line + x_other
    total = len(sources) * piece

    sin_t = jnp.sin(observer_angles[0])
    directions = jnp.stack(
        [sin_t * jnp.cos(observer_angles[1]), sin_t * jnp.sin(observer_angles[1]), jnp.cos(observer_angles[0])]
    )
    directions = directions.reshape(3, nrows * ncols, each).transpose(1, 0, 2)

    modes = (blades * harmonic).reshape(1, -1)
    base = call(local_kernel, jax.ShapeDtypeStruct((piece, width), F32), name="near_and_incident")(
        krylov, geometry, corr_index, corr_weight, modes
    )

    feature = jax.ShapeDtypeStruct((DEPTH, total), BF16)
    columns = call(
        functools.partial(columns_kernel, len(sources)),
        (feature,) * 3,
        [pltpu.VMEM((8, piece), F32)],
        name="column_features",
    )(*sources)

    tile = jax.ShapeDtypeStruct((rows, total), BF16)
    held = []
    for mask, geom in zip([0] + plane_masks, geom_plane):
        at = (row_at ^ mask) * ncols + col_at
        dirs = lax.dynamic_index_in_dim(directions, at, 0, keepdims=False)
        buf = [pltpu.VMEM((rows, CHUNK), F32)] * 2 + [pltpu.VMEM((piece, CHUNK), F32)]
        held.append(
            call(
                functools.partial(tiles_kernel, mask == 0, soft_sq),
                (tile, tile),
                [pltpu.VMEM((rows, DEPTH), BF16)] * 2
                + [pltpu.VMEM((piece, DEPTH), BF16), pltpu.VMEM((8, piece), F32), pltpu.VMEM((8, each), F32)]
                + buf * 2,
                name="tiles",
                cost=pl.CostEstimate(flops=40 * rows * total, bytes_accessed=4 * rows * total, transcendentals=2 * rows * total),
            )(geom, dirs, *columns)
        )

    got = []
    for mask, (t_re, t_im) in list(zip([0] + plane_masks, held))[::-1]:
        dtype = F32 if mask == 0 else BF16
        partial = call(
            functools.partial(apply_kernel, len(vectors), dtype),
            jax.ShapeDtypeStruct((rows, width), dtype),
            name="apply",
            cost=pl.CostEstimate(flops=4 * rows * total * width, bytes_accessed=4 * rows * total, transcendentals=0),
        )(t_re, t_im, *vectors)
        got.append(partial if mask == 0 else xor_permute(partial, "rows", mask))

    return call(
        functools.partial(final_kernel, len(got) - 1),
        (jax.ShapeDtypeStruct((piece, width), F32), jax.ShapeDtypeStruct((each, width), F32)),
        name="combine",
    )(base, got[-1], *got[:-1])


def solution(mesh):
    placed = (
        P(("rows", "cols"), None),
        P(None, ("rows", "cols")),
        P(None, ("rows", "cols")),
        P(None, ("rows", "cols")),
        P(),
        P(),
        P(),
    )
    return jax.shard_map(
        local,
        mesh=mesh,
        in_specs=placed,
        out_specs=(P(("rows", "cols"), None), P(("rows", "cols"), None)),
        check_vma=False,
    )
```

```python
import functools
import math

import jax
import jax.numpy as jnp
from jax import lax
from jax.experimental import pallas as pl
from jax.experimental.pallas import tpu as pltpu
from jax.sharding import PartitionSpec as P

NS = 64
wavenumber = 20.0
cycle_radius = 0.7
cycle_height = 1.0
four_pi = 4.0 * math.pi
two_pi = 2.0 * math.pi

COARSE_D = (-4.203673078505327, 0.9884209687656514)
COARSE_N = (-2.9883226762430346, 3.1051740325541175)
FINE_D = (-2.7704097493600783, 0.6301024476540067)
FINE_N = (0.21837236917008357, -2.1911377274692434, 1.9795254225510943)
ROUNDER = 12582912.0

turns_sq = (wavenumber / two_pi) ** 2
tile_scale = wavenumber**3 / four_pi / two_pi**2
DEPTH = 48
CHUNK = 256
SUB = 16
BF16 = jnp.bfloat16
F32 = jnp.float32


def half_tangent(turn, fine=False):
    f = turn - ((turn + ROUNDER) - ROUNDER)
    z = f * f
    if fine:
        d = (z + FINE_D[0]) * z + FINE_D[1]
        x = f * ((z * FINE_N[0] + FINE_N[1]) * z + FINE_N[2])
    else:
        d = (z + COARSE_D[0]) * z + COARSE_D[1]
        x = f * (z * COARSE_N[0] + COARSE_N[1])
    return d, x


def cos_sin(turn):
    d, x = half_tangent(turn, fine=True)
    q = 1.0 / (d * d + x * x)
    return (d * d - x * x) * q, 2.0 * d * x * q


def parts(v):
    high = v.astype(BF16).astype(F32)
    rest = v - high
    mid = rest.astype(BF16).astype(F32)
    return high, mid, rest - mid


def payload_kernel(masks, x_hbm, g_hbm, angle_hbm, out, dirs_out, vec, x_buf, angles, sem):
    piece = x_hbm.shape[0]
    each = angles.shape[1] // (lax.axis_size("rows") * lax.axis_size("cols"))
    copies = [
        pltpu.make_async_copy(src, dst, sem.at[i])
        for i, (src, dst) in enumerate(((g_hbm, vec), (angle_hbm, angles), (x_hbm, x_buf)))
    ]
    for copy in copies:
        copy.start()
    copies[0].wait()
    g = jnp.concatenate([vec[...], jnp.zeros((1, vec.shape[1]), F32)], axis=0)
    high, mid, low = parts(g)
    out[piece : piece + 16] = jnp.concatenate([high, mid], axis=0).astype(BF16)
    out[piece + 16 : piece + 32] = jnp.concatenate([low, jnp.zeros_like(low)], axis=0).astype(BF16)
    copies[1].wait()
    dirs_out[...] = jnp.zeros_like(dirs_out)
    for i, mask in enumerate(masks):
        owner = (lax.axis_index("rows") ^ mask) * lax.axis_size("cols") + lax.axis_index("cols")
        for j, value in enumerate(directions(angles, owner, each)):
            dirs_out[8 * i + j : 8 * i + j + 1] = value
    copies[2].wait()
    out[0:piece] = x_buf[...]


def shard_features(shard, at, out_s, out_u, out_w, out_x, vec):
    piece = shard.shape[0] - 32
    half = out_x.shape[1] // 2
    x = shard[0:piece]
    out_x[2 * at * piece : (2 * at + 1) * piece] = x
    turned = jnp.concatenate([-x[:, half:], x[:, :half]], axis=1)
    out_x[(2 * at + 1) * piece : (2 * at + 2) * piece] = turned
    held = shard[piece : piece + 32].astype(F32)
    g = held[0:8] + held[8:16] + held[16:24]
    where = pl.ds(at * piece, piece)
    x, y, z = g[0:1], g[1:2], g[2:3] - 1.0
    area = g[6:7] * tile_scale
    zero = jnp.zeros((4, piece), F32)
    vec[0:1], vec[1:2], vec[2:3] = x, y, z
    vec[3:4] = jnp.ones((1, piece), F32)
    vec[4:8] = zero
    vec[4:5] = turns_sq * (x * x + y * y + z * z)
    put_columns(out_s, where, vec[...])
    vec[0:3] = area * g[3:6]
    vec[3:4] = -area * (x * g[3:4] + y * g[4:5] + z * g[5:6])
    vec[4:8] = zero
    put_columns(out_u, where, vec[...])
    vec[0:1], vec[1:2], vec[2:3] = area * x, area * y, area * z
    vec[3:4] = area
    put_columns(out_w, where, vec[...])


def pack_kernel(count, *refs):
    packed = refs[count]
    size = refs[0].shape[0]
    for at in range(count):
        packed[at * size : (at + 1) * size] = refs[at][...]


def columns_kernel(size, count, *refs):
    shards = []
    for ref in refs[:count]:
        shards += [ref.at[at : at + size] for at in range(0, ref.shape[0], size)]
    for at, shard in enumerate(shards):
        shard_features(shard, at, *refs[count:])


def put_columns(out, where, v):
    high, mid, low = parts(v)
    out[0:16, where] = jnp.concatenate([high, mid], axis=0).astype(BF16)
    out[16:32, where] = jnp.concatenate([high, low], axis=0).astype(BF16)
    out[32:48, where] = jnp.concatenate([high, mid], axis=0).astype(BF16)


def row_part(v):
    high, mid, low = parts(v)
    stacked = jnp.concatenate([high, high, mid, high, low, mid], axis=0)
    return stacked.T.astype(BF16)


def row_features(g, dirs, soft_sq, out_s, out_u, out_w, vec, small):
    piece = g.shape[1]
    each = small.shape[1]
    x, y, z = g[0:1], g[1:2], g[2:3] - 1.0
    zero = jnp.zeros((4, piece), F32)
    vec[4:8] = zero
    vec[0:1], vec[1:2], vec[2:3] = (-2.0 * turns_sq) * x, (-2.0 * turns_sq) * y, (-2.0 * turns_sq) * z
    vec[3:4] = turns_sq * (x * x + y * y + z * z + soft_sq)
    vec[4:5] = jnp.ones((1, piece), F32)
    out_s[0:piece] = row_part(vec[...])
    vec[0:1], vec[1:2], vec[2:3] = x, y, z
    vec[3:4] = jnp.ones((1, piece), F32)
    vec[4:8] = zero
    out_u[0:piece] = row_part(vec[...])
    vec[0:3] = g[3:6] * (1.0 / wavenumber)
    vec[3:4] = (x * g[3:4] + y * g[4:5] + z * g[5:6]) * (-1.0 / wavenumber)
    out_w[...] = row_part(vec[...])
    dir_x, dir_y, dir_z = dirs
    small[4:8] = jnp.zeros((4, each), F32)
    small[0:1], small[1:2], small[2:3] = (value * (-wavenumber / two_pi) for value in dirs)
    small[3:4] = dir_z * (-wavenumber / two_pi)
    out_s[piece:] = row_part(small[...])
    small[0:1], small[1:2], small[2:3] = (value * (wavenumber / tile_scale) for value in dirs)
    small[3:4] = jnp.zeros((1, each), F32)
    out_u[piece:] = row_part(small[...])


def directions(angle_ref, owner, each):
    lanes = max(each, 128)
    fit = lanes // each
    window = angle_ref[:, pl.ds(pl.multiple_of(owner // fit * lanes, lanes), lanes)]
    angles = window[:, :each]
    for k in range(1, fit):
        angles = jnp.where(lax.rem(owner, fit) == k, window[:, k * each : (k + 1) * each], angles)
    c, s = cos_sin(angles * (1.0 / two_pi))
    sin_t = s[0:1]
    return sin_t * c[1:2], sin_t * s[1:2], c[0:1]


def panel_entries(s, u, w):
    inverse = lax.rsqrt(s)
    d, x = half_tangent(s * inverse)
    d2, x2 = d * d, x * x
    q = pl.reciprocal((d2 + x2) * s)
    re = (d2 - x2) * q
    h = d * q
    im = (h + h) * x
    p = inverse * (1.0 / two_pi)
    a = p * u + w
    b = p * w - u
    return re * a - im * b, re * b + im * a


def far_entries(turn, scale):
    d, x = half_tangent(turn)
    d2, x2 = d * d, x * x
    q = scale * pl.reciprocal(d2 + x2)
    h = d * q
    return (h + h) * x, (x2 - d2) * q


def tiles_kernel(at_mask, masked, soft_sq, resume, *refs):
    if resume:
        before, rs, ru, rw, cs, cu, cw, x_ref, out, acc, *bufs = refs
        piece = rw.shape[0]
    else:
        g_ref, dirs_ref, cs, cu, cw, x_ref, out, rs, ru, rw, vec, small, acc, *bufs = refs
        piece = g_ref.shape[1]
        dirs = [dirs_ref[8 * at_mask + j : 8 * at_mask + j + 1] for j in range(3)]
        row_features(g_ref[...], dirs, soft_sq, rs, ru, rw, vec, small)
    rows = out.shape[0]
    count = cs.shape[1] // CHUNK

    def multiply(at, buf):
        where = pl.ds(pl.multiple_of(at * CHUNK, CHUNK), CHUNK)
        for row_ref, col_ref, hold in ((rs, cs, buf[0]), (ru, cu, buf[1]), (rw, cw, buf[2])):
            hold[...] = jnp.dot(row_ref[...], col_ref[:, where], preferred_element_type=F32)

    def entries(buf, tile, diagonal=None):
        for begin in range(0, rows, SUB):
            take = pl.ds(begin, SUB)
            if begin < piece:
                re, im = panel_entries(buf[0][take], buf[1][take], buf[2][take])
                if diagonal is not None:
                    down = lax.broadcasted_iota(jnp.int32, (SUB, CHUNK), 0) + begin
                    across = lax.broadcasted_iota(jnp.int32, (SUB, CHUNK), 1) + diagonal
                    re = jnp.where(down == across, 0.0, re)
                    im = jnp.where(down == across, 0.0, im)
            else:
                re, im = far_entries(buf[0][take], buf[1][take])
            tile[take, :CHUNK] = re.astype(BF16)
            tile[take, CHUNK:] = im.astype(BF16)

    def apply(at, tile, begin=False):
        where = pl.ds(pl.multiple_of(at * 2 * CHUNK, 2 * CHUNK), 2 * CHUNK)
        product = jnp.dot(tile[...], x_ref[where], preferred_element_type=F32)
        if not begin:
            acc[...] += product
        elif resume:
            acc[...] = before[...] + product
        else:
            acc[...] = product

    first, second, tile_a, tile_b = bufs[:3], bufs[3:6], bufs[6], bufs[7]
    multiply(0, first)

    def two(step, begin, last):
        own = last and masked
        multiply(2 * step + 1, second)
        if not begin:
            apply(2 * step - 1, tile_b)
        entries(first, tile_a, 0 if own and piece == 2 * CHUNK else None)
        if not last:
            multiply(2 * step + 2, first)
        apply(2 * step, tile_a, begin)
        entries(second, tile_b, piece - CHUNK if own else None)

    def body(step, carry):
        two(step, False, False)
        return carry

    steps = count // 2
    two(0, True, steps == 1)
    if steps > 1:
        lax.fori_loop(1, steps - 1, body, 0)
        two(steps - 1, False, True)
    apply(count - 1, tile_b)
    out[...] = acc[...].astype(out.dtype)


def dot_first(left, right, precision=None):
    return lax.dot_general(
        left, right, (((0,), (0,)), ((), ())), precision=precision, preferred_element_type=F32
    )


def local_kernel(x_ref, g_ref, index_ref, weight_ref, blade_ref, harmonic_ref, out):
    piece, width = x_ref.shape
    half = width // 2
    count = index_ref.shape[0]
    rows = lax.axis_index("rows")
    cols = lax.axis_index("cols")
    base = (rows * lax.axis_size("cols") + cols) * piece
    ids = lax.broadcasted_iota(jnp.int32, (piece, piece), 0) + base
    m_re = jnp.zeros((piece, piece), F32)
    m_im = jnp.zeros((piece, piece), F32)
    for c in range(count):
        hit = ids == index_ref[c : c + 1]
        m_re += jnp.where(hit, weight_ref[c : c + 1], 0.0)
        m_im += jnp.where(hit, weight_ref[count + c : count + c + 1], 0.0)
    x = x_ref[...]
    first = jnp.zeros((piece, width), F32)
    second = jnp.zeros((piece, width), F32)
    for part in parts(m_re):
        first += dot_first(part.astype(BF16), x)
    for part in parts(m_im):
        second += dot_first(part.astype(BF16), x)
    g = g_ref[...]
    source = lax.broadcasted_iota(jnp.int32, (NS, 1), 0)
    src_cos, src_sin = cos_sin(source.astype(F32) * (1.0 / NS))
    dx = g[0:1] - cycle_radius * src_cos
    dy = g[1:2] - cycle_radius * src_sin
    dz = g[2:3] - cycle_height
    r_sq = dx * dx + dy * dy + dz * dz
    inverse = lax.rsqrt(r_sq)
    c, s = cos_sin(r_sq * inverse * (wavenumber / two_pi))
    g_re = c * inverse * (1.0 / four_pi)
    g_im = s * inverse * (1.0 / four_pi)
    slope = (dx * g[3:4] + dy * g[4:5] + dz * g[5:6]) * inverse
    f_re = 1.0 - slope
    f_im = slope * inverse * (-1.0 / wavenumber)
    h_re = g_re * f_re - g_im * f_im
    h_im = g_re * f_im + g_im * f_re
    turn = lax.rem(source * (blade_ref[...] * harmonic_ref[...]), NS).astype(F32) * (1.0 / NS)
    e_re, e_im = cos_sin(turn)
    lhs = jnp.concatenate([h_re, h_im], axis=0)
    rhs = jnp.concatenate(
        [jnp.concatenate([e_re, e_im], axis=1), jnp.concatenate([-e_im, e_re], axis=1)], axis=0
    )
    b = dot_first(lhs, rhs, lax.Precision.HIGHEST)
    xf = x.astype(F32)
    out[:, :half] = b[:, :half] - 0.5 * xf[:, :half] - (first[:, :half] - second[:, half:])
    out[:, half:] = b[:, half:] - 0.5 * xf[:, half:] - (first[:, half:] + second[:, :half])


def final_kernel(count, base, own, *refs):
    got, residual, far = refs[:count], refs[count], refs[count + 1]
    piece = residual.shape[0]
    total = own[...]
    for ref in got:
        total += ref[...].astype(F32)
    residual[...] = base[...] - total[:piece]
    far[...] = total[piece:]


def call(kernel, out_shape, scratch=(), name=None, cost=None, inputs=None, limit=40):
    return pl.pallas_call(
        kernel,
        out_shape=out_shape,
        scratch_shapes=list(scratch),
        compiler_params=pltpu.CompilerParams(vmem_limit_bytes=limit * 2**20),
        cost_estimate=cost,
        name=name,
        **({} if inputs is None else {"in_specs": inputs}),
    )


def TILE_COST(entries):
    return pl.CostEstimate(flops=4 * entries, bytes_accessed=entries, transcendentals=0)


NEAR_COST = pl.CostEstimate(flops=10**7, bytes_accessed=10**6, transcendentals=10**5)


def xor_permute(value, axis, mask):
    size = lax.axis_size(axis)
    return lax.ppermute(value, axis, [(i, i ^ mask) for i in range(size)])


def local(krylov, geometry, corr_index, corr_weight, blades, harmonic, observer_angles):
    nrows = lax.axis_size("rows")
    ncols = lax.axis_size("cols")
    piece, width = krylov.shape
    soft_sq = 4.0 / (piece * nrows * ncols)
    each = observer_angles.shape[1] // (nrows * ncols)
    rows = piece + each

    masks = list(range(2, nrows, 2))
    order = [0] + masks
    payload, dirs = call(
        functools.partial(payload_kernel, order),
        (
            jax.ShapeDtypeStruct((piece + 32, width), BF16),
            jax.ShapeDtypeStruct((8 * len(order), each), F32),
        ),
        [pltpu.VMEM(a.shape, a.dtype) for a in (geometry, krylov, observer_angles)] + [pltpu.SemaphoreType.DMA((3,))],
        name="payload",
        inputs=[pl.BlockSpec(memory_space=pltpu.HBM)] * 3,
        limit=64,
    )(krylov, geometry, observer_angles)
    line = [payload] + [xor_permute(payload, "cols", m) for m in range(1, ncols)]
    near_half, far_half = line[: ncols // 2][::-1], line[ncols // 2 :]

    plane = {m: xor_permute(geometry, "rows", m) for m in masks}

    base = call(
        local_kernel,
        jax.ShapeDtypeStruct((piece, width), F32),
        name="near_and_incident",
        cost=NEAR_COST,
    )(krylov, geometry, corr_index, corr_weight, blades.reshape(1, -1), harmonic.reshape(1, -1))

    def exchange(shards):
        packed = call(
            functools.partial(pack_kernel, len(shards)),
            jax.ShapeDtypeStruct((len(shards) * (piece + 32), width), BF16),
            name="pack",
        )(*shards)
        return xor_permute(packed, "rows", 1)

    def features(*shards):
        panels = sum(shard.shape[0] for shard in shards) // (piece + 32) * piece
        feature = jax.ShapeDtypeStruct((DEPTH, panels), BF16)
        return call(
            functools.partial(columns_kernel, piece + 32, len(shards)),
            (feature, feature, feature, jax.ShapeDtypeStruct((2 * panels, width), BF16)),
            [pltpu.VMEM((8, piece), F32)],
            name="columns",
        )(*shards)

    def buffers():
        buf = [pltpu.VMEM((rows, CHUNK), F32)] * 2 + [pltpu.VMEM((piece, CHUNK), F32)]
        return [pltpu.VMEM((rows, width), F32)] + buf * 2 + [pltpu.VMEM((rows, 2 * CHUNK), BF16)] * 2

    def tiles(mask, columns, geom):
        return call(
            functools.partial(tiles_kernel, order.index(mask), mask == 0, soft_sq, False),
            (
                jax.ShapeDtypeStruct((rows, width), F32),
                jax.ShapeDtypeStruct((rows, DEPTH), BF16),
                jax.ShapeDtypeStruct((rows, DEPTH), BF16),
                jax.ShapeDtypeStruct((piece, DEPTH), BF16),
            ),
            [pltpu.VMEM((8, piece), F32), pltpu.VMEM((8, each), F32)] + buffers(),
            name="tiles",
            cost=TILE_COST(rows * columns[0].shape[1]),
        )(geom, dirs, *columns)

    def resume(mask, columns, before):
        return call(
            functools.partial(tiles_kernel, 0, False, soft_sq, True),
            jax.ShapeDtypeStruct((rows, width), BF16 if mask else F32),
            buffers(),
            name="resume",
            cost=TILE_COST(rows * columns[0].shape[1]),
        )(*before, *columns)

    early = {m: plane[m] for m in masks[:2]}
    received, dirs, early = lax.optimization_barrier((near_half[:-1], dirs, early))
    plane.update(early)
    near_half = received + near_half[-1:]
    columns = features(*near_half)
    held = {0: tiles(0, columns, geometry)}
    held[0], plane = lax.optimization_barrier((held[0], plane))
    for m in masks:
        held[m] = tiles(m, columns, plane[m])

    first = order[:-1]
    far_half, done = lax.optimization_barrier((far_half, [held[m] for m in first]))
    held.update(zip(first, done))
    packed = exchange(near_half + far_half)
    packed, held[masks[-1]] = lax.optimization_barrier((packed, held[masks[-1]]))
    columns = features(packed, *far_half)
    got = [xor_permute(resume(m, columns, held[m]), "rows", m) for m in masks[::-1]]
    got[:-1], held[0] = lax.optimization_barrier((got[:-1], held[0]))
    own = resume(0, columns, held[0])

    return call(
        functools.partial(final_kernel, len(got)),
        (jax.ShapeDtypeStruct((piece, width), F32), jax.ShapeDtypeStruct((each, width), F32)),
        name="combine",
    )(base, own, *got)


def solution(mesh):
    placed = (
        P(("rows", "cols"), None),
        P(None, ("rows", "cols")),
        P(None, ("rows", "cols")),
        P(None, ("rows", "cols")),
        P(),
        P(),
        P(),
    )
    return jax.shard_map(
        local,
        mesh=mesh,
        in_specs=placed,
        out_specs=(P(("rows", "cols"), None), P(("rows", "cols"), None)),
        check_vma=False,
    )
```

```python
import functools
import math

import jax
import jax.numpy as jnp
from jax import lax
from jax.experimental import pallas as pl
from jax.experimental.pallas import tpu as pltpu
from jax.sharding import PartitionSpec as P

NS = 64
wavenumber = 20.0
cycle_radius = 0.7
cycle_height = 1.0
four_pi = 4.0 * math.pi
two_pi = 2.0 * math.pi

COARSE_D = (-4.203673078505327, 0.9884209687656514)
COARSE_N = (-2.9883226762430346, 3.1051740325541175)
FINE_D = (-2.7704097493600783, 0.6301024476540067)
FINE_N = (0.21837236917008357, -2.1911377274692434, 1.9795254225510943)
ROUNDER = 12582912.0

turns_sq = (wavenumber / two_pi) ** 2
tile_scale = wavenumber**3 / four_pi / two_pi**2
DEPTH = 48
CHUNK = 256
SUB = 16
BF16 = jnp.bfloat16
F32 = jnp.float32


def half_tangent(turn, fine=False):
    f = turn - ((turn + ROUNDER) - ROUNDER)
    z = f * f
    if fine:
        d = (z + FINE_D[0]) * z + FINE_D[1]
        x = f * ((z * FINE_N[0] + FINE_N[1]) * z + FINE_N[2])
    else:
        d = (z + COARSE_D[0]) * z + COARSE_D[1]
        x = f * (z * COARSE_N[0] + COARSE_N[1])
    return d, x


def cos_sin(turn):
    d, x = half_tangent(turn, fine=True)
    q = 1.0 / (d * d + x * x)
    return (d * d - x * x) * q, 2.0 * d * x * q


def parts(v):
    high = v.astype(BF16).astype(F32)
    rest = v - high
    mid = rest.astype(BF16).astype(F32)
    return high, mid, rest - mid


def payload_kernel(masks, x_hbm, g_hbm, angle_hbm, out, dirs_out, vec, x_buf, angles, sem):
    piece = x_hbm.shape[0]
    each = angles.shape[1] // (lax.axis_size("rows") * lax.axis_size("cols"))
    copies = [
        pltpu.make_async_copy(src, dst, sem.at[i])
        for i, (src, dst) in enumerate(((g_hbm, vec), (angle_hbm, angles), (x_hbm, x_buf)))
    ]
    for copy in copies:
        copy.start()
    copies[0].wait()
    g = jnp.concatenate([vec[...], jnp.zeros((1, vec.shape[1]), F32)], axis=0)
    high, mid, low = parts(g)
    out[piece : piece + 16] = jnp.concatenate([high, mid], axis=0).astype(BF16)
    out[piece + 16 : piece + 32] = jnp.concatenate([low, jnp.zeros_like(low)], axis=0).astype(BF16)
    copies[1].wait()
    dirs_out[...] = jnp.zeros_like(dirs_out)
    for i, mask in enumerate(masks):
        owner = (lax.axis_index("rows") ^ mask) * lax.axis_size("cols") + lax.axis_index("cols")
        for j, value in enumerate(directions(angles, owner, each)):
            dirs_out[8 * i + j : 8 * i + j + 1] = value
    copies[2].wait()
    out[0:piece] = x_buf[...]


def shard_features(shard, at, out_s, out_u, out_w, out_x, vec):
    piece = shard.shape[0] - 32
    half = out_x.shape[1] // 2
    x = shard[0:piece]
    out_x[2 * at * piece : (2 * at + 1) * piece] = x
    turned = jnp.concatenate([-x[:, half:], x[:, :half]], axis=1)
    out_x[(2 * at + 1) * piece : (2 * at + 2) * piece] = turned
    held = shard[piece : piece + 32].astype(F32)
    g = held[0:8] + held[8:16] + held[16:24]
    where = pl.ds(at * piece, piece)
    x, y, z = g[0:1], g[1:2], g[2:3] - 1.0
    area = g[6:7] * tile_scale
    zero = jnp.zeros((4, piece), F32)
    vec[0:1], vec[1:2], vec[2:3] = x, y, z
    vec[3:4] = jnp.ones((1, piece), F32)
    vec[4:8] = zero
    vec[4:5] = turns_sq * (x * x + y * y + z * z)
    put_columns(out_s, where, vec[...])
    vec[0:3] = area * g[3:6]
    vec[3:4] = -area * (x * g[3:4] + y * g[4:5] + z * g[5:6])
    vec[4:8] = zero
    put_columns(out_u, where, vec[...])
    vec[0:1], vec[1:2], vec[2:3] = area * x, area * y, area * z
    vec[3:4] = area
    put_columns(out_w, where, vec[...])


def pack_kernel(count, *refs):
    packed = refs[count]
    size = refs[0].shape[0]
    for at in range(count):
        packed[at * size : (at + 1) * size] = refs[at][...]


def columns_kernel(size, count, *refs):
    shards = []
    for ref in refs[:count]:
        shards += [ref.at[at : at + size] for at in range(0, ref.shape[0], size)]
    for at, shard in enumerate(shards):
        shard_features(shard, at, *refs[count:])


def put_columns(out, where, v):
    high, mid, low = parts(v)
    out[0:16, where] = jnp.concatenate([high, mid], axis=0).astype(BF16)
    out[16:32, where] = jnp.concatenate([high, low], axis=0).astype(BF16)
    out[32:48, where] = jnp.concatenate([high, mid], axis=0).astype(BF16)


def row_part(v):
    high, mid, low = parts(v)
    stacked = jnp.concatenate([high, high, mid, high, low, mid], axis=0)
    return stacked.T.astype(BF16)


def row_features(g, dirs, soft_sq, out_s, out_u, out_w, vec, small):
    piece = g.shape[1]
    each = small.shape[1]
    x, y, z = g[0:1], g[1:2], g[2:3] - 1.0
    zero = jnp.zeros((4, piece), F32)
    vec[4:8] = zero
    vec[0:1], vec[1:2], vec[2:3] = (-2.0 * turns_sq) * x, (-2.0 * turns_sq) * y, (-2.0 * turns_sq) * z
    vec[3:4] = turns_sq * (x * x + y * y + z * z + soft_sq)
    vec[4:5] = jnp.ones((1, piece), F32)
    out_s[0:piece] = row_part(vec[...])
    vec[0:1], vec[1:2], vec[2:3] = x, y, z
    vec[3:4] = jnp.ones((1, piece), F32)
    vec[4:8] = zero
    out_u[0:piece] = row_part(vec[...])
    vec[0:3] = g[3:6] * (1.0 / wavenumber)
    vec[3:4] = (x * g[3:4] + y * g[4:5] + z * g[5:6]) * (-1.0 / wavenumber)
    out_w[...] = row_part(vec[...])
    dir_x, dir_y, dir_z = dirs
    small[4:8] = jnp.zeros((4, each), F32)
    small[0:1], small[1:2], small[2:3] = (value * (-wavenumber / two_pi) for value in dirs)
    small[3:4] = dir_z * (-wavenumber / two_pi)
    out_s[piece:] = row_part(small[...])
    small[0:1], small[1:2], small[2:3] = (value * (wavenumber / tile_scale) for value in dirs)
    small[3:4] = jnp.zeros((1, each), F32)
    out_u[piece:] = row_part(small[...])


def directions(angle_ref, owner, each):
    lanes = max(each, 128)
    fit = lanes // each
    window = angle_ref[:, pl.ds(pl.multiple_of(owner // fit * lanes, lanes), lanes)]
    angles = window[:, :each]
    for k in range(1, fit):
        angles = jnp.where(lax.rem(owner, fit) == k, window[:, k * each : (k + 1) * each], angles)
    c, s = cos_sin(angles * (1.0 / two_pi))
    sin_t = s[0:1]
    return sin_t * c[1:2], sin_t * s[1:2], c[0:1]


def panel_entries(s, u, w):
    inverse = lax.rsqrt(s)
    d, x = half_tangent(s * inverse)
    d2, x2 = d * d, x * x
    q = pl.reciprocal((d2 + x2) * s)
    re = (d2 - x2) * q
    h = d * q
    im = (h + h) * x
    p = inverse * (1.0 / two_pi)
    a = p * u + w
    b = p * w - u
    return re * a - im * b, re * b + im * a


def far_entries(turn, scale):
    d, x = half_tangent(turn)
    d2, x2 = d * d, x * x
    q = scale * pl.reciprocal(d2 + x2)
    h = d * q
    return (h + h) * x, (x2 - d2) * q


def tiles_kernel(soft_sq, resume, picks, skip, *refs):
    count = len(picks)
    if resume:
        befores, refs = refs[:count], refs[count:]
        keeps, refs = refs[: 3 * count], refs[3 * count :]
        cs, cu, cw, x_ref, *refs = refs
        outs, bufs = refs[:count], refs[count:]
    else:
        geoms, refs = refs[:count], refs[count:]
        dirs_ref, cs, cu, cw, x_ref, *refs = refs
        keeps, refs = refs[: 3 * count], refs[3 * count :]
        outs, (vec, small, *bufs) = refs[:count], refs[count:]
    rows, width = keeps[0].shape[0], x_ref.shape[1]
    piece = keeps[2].shape[0]
    steps = (cs.shape[1] // CHUNK - skip) // 2
    first, second, tile_a, tile_b, acc = bufs[:3], bufs[3:6], bufs[6], bufs[7], bufs[8]

    def prepare(index):
        if not resume:
            at = 8 * picks[index]
            dirs = [dirs_ref[at + j : at + j + 1] for j in range(3)]
            row_features(geoms[index][...], dirs, soft_sq, *keeps[3 * index : 3 * index + 3], vec, small)

    def multiply(index, at, buf):
        where = pl.ds(pl.multiple_of((at + skip) * CHUNK, CHUNK), CHUNK)
        for row_ref, col_ref, hold in zip(keeps[3 * index : 3 * index + 3], (cs, cu, cw), buf):
            hold[...] = jnp.dot(row_ref[...], col_ref[:, where], preferred_element_type=F32)

    def entries(buf, tile, diagonal=None):
        for begin in range(0, rows, SUB):
            take = pl.ds(begin, SUB)
            if begin < piece:
                re, im = panel_entries(buf[0][take], buf[1][take], buf[2][take])
                if diagonal is not None:
                    down = lax.broadcasted_iota(jnp.int32, (SUB, CHUNK), 0) + begin
                    across = lax.broadcasted_iota(jnp.int32, (SUB, CHUNK), 1) + diagonal
                    re = jnp.where(down == across, 0.0, re)
                    im = jnp.where(down == across, 0.0, im)
            else:
                re, im = far_entries(buf[0][take], buf[1][take])
            tile[take, :CHUNK] = re.astype(BF16)
            tile[take, CHUNK:] = im.astype(BF16)

    def apply(index, at, tile, begin=False, end=False):
        where = pl.ds(pl.multiple_of((at + skip) * 2 * CHUNK, 2 * CHUNK), 2 * CHUNK)
        product = jnp.dot(tile[...], x_ref[where], preferred_element_type=F32)
        if not begin:
            product = acc[...] + product
        elif resume:
            product = befores[index][...] + product
        if end:
            outs[index][...] = product.astype(outs[index].dtype)
        else:
            acc[...] = product

    def two(index, step, begin, last):
        own = last and not resume and picks[index] == 0
        multiply(index, 2 * step + 1, second)
        if not begin:
            apply(index, 2 * step - 1, tile_b)
        elif index:
            apply(index - 1, 2 * steps - 1, tile_b, end=True)
        entries(first, tile_a, 0 if own and piece == 2 * CHUNK else None)
        if not last:
            multiply(index, 2 * step + 2, first)
        elif index + 1 < len(picks):
            prepare(index + 1)
            multiply(index + 1, 0, first)
        apply(index, 2 * step, tile_a, begin)
        entries(second, tile_b, piece - CHUNK if own else None)

    def body(index, step, carry):
        two(index, step, False, False)
        return carry

    prepare(0)
    multiply(0, 0, first)
    for index in range(len(picks)):
        two(index, 0, True, steps == 1)
        if steps > 1:
            lax.fori_loop(1, steps - 1, functools.partial(body, index), 0)
            two(index, steps - 1, False, True)
    apply(len(picks) - 1, 2 * steps - 1, tile_b, end=True)


def dot_first(left, right, precision=None):
    return lax.dot_general(
        left, right, (((0,), (0,)), ((), ())), precision=precision, preferred_element_type=F32
    )


def local_kernel(x_ref, g_ref, index_ref, weight_ref, blade_ref, harmonic_ref, out):
    piece, width = x_ref.shape
    half = width // 2
    count = index_ref.shape[0]
    rows = lax.axis_index("rows")
    cols = lax.axis_index("cols")
    base = (rows * lax.axis_size("cols") + cols) * piece
    ids = lax.broadcasted_iota(jnp.int32, (piece, piece), 0) + base
    m_re = jnp.zeros((piece, piece), F32)
    m_im = jnp.zeros((piece, piece), F32)
    for c in range(count):
        hit = ids == index_ref[c : c + 1]
        m_re += jnp.where(hit, weight_ref[c : c + 1], 0.0)
        m_im += jnp.where(hit, weight_ref[count + c : count + c + 1], 0.0)
    x = x_ref[...]
    first = jnp.zeros((piece, width), F32)
    second = jnp.zeros((piece, width), F32)
    for part in parts(m_re):
        first += dot_first(part.astype(BF16), x)
    for part in parts(m_im):
        second += dot_first(part.astype(BF16), x)
    g = g_ref[...]
    source = lax.broadcasted_iota(jnp.int32, (NS, 1), 0)
    src_cos, src_sin = cos_sin(source.astype(F32) * (1.0 / NS))
    dx = g[0:1] - cycle_radius * src_cos
    dy = g[1:2] - cycle_radius * src_sin
    dz = g[2:3] - cycle_height
    r_sq = dx * dx + dy * dy + dz * dz
    inverse = lax.rsqrt(r_sq)
    c, s = cos_sin(r_sq * inverse * (wavenumber / two_pi))
    g_re = c * inverse * (1.0 / four_pi)
    g_im = s * inverse * (1.0 / four_pi)
    slope = (dx * g[3:4] + dy * g[4:5] + dz * g[5:6]) * inverse
    f_re = 1.0 - slope
    f_im = slope * inverse * (-1.0 / wavenumber)
    h_re = g_re * f_re - g_im * f_im
    h_im = g_re * f_im + g_im * f_re
    turn = lax.rem(source * (blade_ref[...] * harmonic_ref[...]), NS).astype(F32) * (1.0 / NS)
    e_re, e_im = cos_sin(turn)
    lhs = jnp.concatenate([h_re, h_im], axis=0)
    rhs = jnp.concatenate(
        [jnp.concatenate([e_re, e_im], axis=1), jnp.concatenate([-e_im, e_re], axis=1)], axis=0
    )
    b = dot_first(lhs, rhs, lax.Precision.HIGHEST)
    xf = x.astype(F32)
    out[:, :half] = b[:, :half] - 0.5 * xf[:, :half] - (first[:, :half] - second[:, half:])
    out[:, half:] = b[:, half:] - 0.5 * xf[:, half:] - (first[:, half:] + second[:, :half])


def final_kernel(count, base, own, *refs):
    got, residual, far = refs[:count], refs[count], refs[count + 1]
    piece = residual.shape[0]
    total = own[...]
    for ref in got:
        total += ref[...].astype(F32)
    residual[...] = base[...] - total[:piece]
    far[...] = total[piece:]


def call(kernel, out_shape, scratch=(), name=None, cost=None, inputs=None, limit=40):
    return pl.pallas_call(
        kernel,
        out_shape=out_shape,
        scratch_shapes=list(scratch),
        compiler_params=pltpu.CompilerParams(vmem_limit_bytes=limit * 2**20),
        cost_estimate=cost,
        name=name,
        **({} if inputs is None else {"in_specs": inputs}),
    )


def TILE_COST(entries):
    return pl.CostEstimate(flops=1, bytes_accessed=2 * 10**6, transcendentals=0)


NEAR_COST = pl.CostEstimate(flops=1, bytes_accessed=2 * 10**6, transcendentals=0)


def xor_permute(value, axis, mask):
    size = lax.axis_size(axis)
    return lax.ppermute(value, axis, [(i, i ^ mask) for i in range(size)])


def local(krylov, geometry, corr_index, corr_weight, blades, harmonic, observer_angles):
    nrows = lax.axis_size("rows")
    ncols = lax.axis_size("cols")
    piece, width = krylov.shape
    soft_sq = 4.0 / (piece * nrows * ncols)
    each = observer_angles.shape[1] // (nrows * ncols)
    rows = piece + each

    masks = list(range(2, nrows, 2))
    order = [0] + masks
    payload, dirs, geometry_here = call(
        functools.partial(payload_kernel, order),
        (
            pltpu.VMEM((piece + 32, width), BF16),
            pltpu.VMEM((8 * len(order), each), F32),
            pltpu.VMEM(geometry.shape, F32),
        ),
        [pltpu.VMEM(a.shape, a.dtype) for a in (krylov, observer_angles)] + [pltpu.SemaphoreType.DMA((3,))],
        name="payload",
        inputs=[pl.BlockSpec(memory_space=pltpu.HBM)] * 3,
        limit=56,
    )(krylov, geometry, observer_angles)
    line = [payload] + [xor_permute(payload, "cols", m) for m in range(ncols - 1, 0, -1)]
    near_half, far_half = line[: ncols // 2][::-1], line[ncols // 2 :]

    plane = [geometry_here] + [xor_permute(geometry_here, "rows", m) for m in masks]

    def exchange(shards):
        packed = call(
            functools.partial(pack_kernel, len(shards)),
            jax.ShapeDtypeStruct((len(shards) * (piece + 32), width), BF16),
            name="pack",
        )(*shards)
        return xor_permute(packed, "rows", 1)

    def features(*shards):
        panels = sum(shard.shape[0] for shard in shards) // (piece + 32) * piece
        feature = jax.ShapeDtypeStruct((DEPTH, panels), BF16)
        return call(
            functools.partial(columns_kernel, piece + 32, len(shards)),
            (feature, feature, feature, jax.ShapeDtypeStruct((2 * panels, width), BF16)),
            [pltpu.VMEM((8, piece), F32)],
            name="columns",
        )(*shards)

    buf = [pltpu.VMEM((rows, CHUNK), F32)] * 2 + [pltpu.VMEM((piece, CHUNK), F32)]
    buf = buf * 2 + [pltpu.VMEM((rows, 2 * CHUNK), BF16)] * 2 + [pltpu.VMEM((rows, width), F32)]

    partial = jax.ShapeDtypeStruct((rows, width), F32)
    kept = [jax.ShapeDtypeStruct((size, DEPTH), BF16) for size in (rows, rows, piece)]
    held, keeps = {}, {}

    def tiles(picks, columns):
        found = call(
            functools.partial(tiles_kernel, soft_sq, False, picks, 0),
            (*kept * len(picks), *[partial] * len(picks)),
            [pltpu.VMEM((8, piece), F32), pltpu.VMEM((8, each), F32)] + buf,
            name="tiles",
            cost=TILE_COST(rows * columns[0].shape[1]),
        )(*[plane[pick] for pick in picks], dirs, *columns)
        for at, pick in enumerate(picks):
            keeps[pick], held[pick] = found[3 * at : 3 * at + 3], found[3 * len(picks) + at]

    def resume(picks, columns, last=False, skip=0):
        found = call(
            functools.partial(tiles_kernel, soft_sq, True, picks, skip),
            tuple(jax.ShapeDtypeStruct((rows, width), BF16 if pick and last else F32) for pick in picks),
            buf,
            name="resume",
            cost=TILE_COST(rows * columns[0].shape[1]),
        )(*[held[pick] for pick in picks], *[keep for pick in picks for keep in keeps[pick]], *columns)
        held.update(zip(picks, found))

    def after(value, *earlier):
        return lax.optimization_barrier((value, earlier))[0]

    received, dirs, early = lax.optimization_barrier((near_half[:-1], dirs, plane[1:3]))
    plane[1:3] = early
    near_half = received + near_half[-1:]
    columns = features(*near_half)
    final = len(order) - 1
    tiles(list(range(final)), columns)
    plane[final] = after(plane[final], held[0])
    tiles([final], columns)

    packed = exchange(near_half)
    far_half = after(far_half, held)
    other = exchange(far_half)
    ahead = list(range(final, final // 2, -1))
    resume(ahead, features(packed))
    other = after(other, held)
    columns = features(packed, other, *far_half)
    got = []
    for pick in range(final, 0, -1):
        resume([pick], columns, True, 2 * piece * (ncols // 2) // 2 // CHUNK if pick in ahead else 0)
        got.append(xor_permute(held[pick], "rows", order[pick]))
        held[pick - 1] = after(held[pick - 1], held[pick])

    got[:1], held[0] = lax.optimization_barrier((got[:1], held[0]))
    resume([0], columns, True)
    own = held[0]

    got[:-1], near_geometry = lax.optimization_barrier((got[:-1], after(geometry_here, own)))
    base = call(
        local_kernel,
        jax.ShapeDtypeStruct((piece, width), F32),
        name="near_and_incident",
        cost=NEAR_COST,
    )(krylov, near_geometry, corr_index, corr_weight, blades.reshape(1, -1), harmonic.reshape(1, -1))

    return call(
        functools.partial(final_kernel, len(got)),
        (jax.ShapeDtypeStruct((piece, width), F32), jax.ShapeDtypeStruct((each, width), F32)),
        name="combine",
    )(base, own, *got)


def solution(mesh):
    placed = (
        P(("rows", "cols"), None),
        P(None, ("rows", "cols")),
        P(None, ("rows", "cols")),
        P(None, ("rows", "cols")),
        P(),
        P(),
        P(),
    )
    return jax.shard_map(
        local,
        mesh=mesh,
        in_specs=placed,
        out_specs=(P(("rows", "cols"), None), P(("rows", "cols"), None)),
        check_vma=False,
    )
```

```python
import functools
import math

import jax
import jax.numpy as jnp
from jax import lax
from jax.experimental import pallas as pl
from jax.experimental.pallas import tpu as pltpu
from jax.sharding import PartitionSpec as P

NS = 64
wavenumber = 20.0
cycle_radius = 0.7
cycle_height = 1.0
four_pi = 4.0 * math.pi
two_pi = 2.0 * math.pi

COARSE_D = (-4.203673078505327, 0.9884209687656514)
COARSE_N = (-2.9883226762430346, 3.1051740325541175)
FINE_D = (-2.7704097493600783, 0.6301024476540067)
FINE_N = (0.21837236917008357, -2.1911377274692434, 1.9795254225510943)
ROUNDER = 12582912.0

turns_sq = (wavenumber / two_pi) ** 2
tile_scale = wavenumber**3 / four_pi / two_pi**2
DEPTH = 48
CHUNK = 256
SUB = 16
BF16 = jnp.bfloat16
F32 = jnp.float32


def half_tangent(turn, fine=False):
    f = turn - ((turn + ROUNDER) - ROUNDER)
    z = f * f
    if fine:
        d = (z + FINE_D[0]) * z + FINE_D[1]
        x = f * ((z * FINE_N[0] + FINE_N[1]) * z + FINE_N[2])
    else:
        d = (z + COARSE_D[0]) * z + COARSE_D[1]
        x = f * (z * COARSE_N[0] + COARSE_N[1])
    return d, x


def cos_sin(turn):
    d, x = half_tangent(turn, fine=True)
    q = 1.0 / (d * d + x * x)
    return (d * d - x * x) * q, 2.0 * d * x * q


def parts(v):
    high = v.astype(BF16).astype(F32)
    rest = v - high
    mid = rest.astype(BF16).astype(F32)
    return high, mid, rest - mid


def payload_kernel(masks, x_hbm, g_hbm, angle_hbm, out, dirs_out, vec, x_buf, angles, sem):
    piece = x_hbm.shape[0]
    each = angles.shape[1] // (lax.axis_size("rows") * lax.axis_size("cols"))
    copies = [
        pltpu.make_async_copy(src, dst, sem.at[i])
        for i, (src, dst) in enumerate(((g_hbm, vec), (angle_hbm, angles), (x_hbm, x_buf)))
    ]
    for copy in copies:
        copy.start()
    copies[0].wait()
    g = jnp.concatenate([vec[...], jnp.zeros((1, vec.shape[1]), F32)], axis=0)
    high, mid, low = parts(g)
    out[piece : piece + 16] = jnp.concatenate([high, mid], axis=0).astype(BF16)
    out[piece + 16 : piece + 32] = jnp.concatenate([low, jnp.zeros_like(low)], axis=0).astype(BF16)
    copies[1].wait()
    dirs_out[...] = jnp.zeros_like(dirs_out)
    for i, mask in enumerate(masks):
        owner = (lax.axis_index("rows") ^ mask) * lax.axis_size("cols") + lax.axis_index("cols")
        for j, value in enumerate(directions(angles, owner, each)):
            dirs_out[8 * i + j : 8 * i + j + 1] = value
    copies[2].wait()
    out[0:piece] = x_buf[...]


def shard_features(shard, at, out_s, out_u, out_w, out_x, vec):
    piece = shard.shape[0] - 32
    half = out_x.shape[1] // 2
    x = shard[0:piece]
    out_x[2 * at * piece : (2 * at + 1) * piece] = x
    turned = jnp.concatenate([-x[:, half:], x[:, :half]], axis=1)
    out_x[(2 * at + 1) * piece : (2 * at + 2) * piece] = turned
    held = shard[piece : piece + 32].astype(F32)
    g = held[0:8] + held[8:16] + held[16:24]
    where = pl.ds(at * piece, piece)
    x, y, z = g[0:1], g[1:2], g[2:3] - 1.0
    area = g[6:7] * tile_scale
    zero = jnp.zeros((4, piece), F32)
    vec[0:1], vec[1:2], vec[2:3] = x, y, z
    vec[3:4] = jnp.ones((1, piece), F32)
    vec[4:8] = zero
    vec[4:5] = turns_sq * (x * x + y * y + z * z)
    put_columns(out_s, where, vec[...])
    vec[0:3] = area * g[3:6]
    vec[3:4] = -area * (x * g[3:4] + y * g[4:5] + z * g[5:6])
    vec[4:8] = zero
    put_columns(out_u, where, vec[...])
    vec[0:1], vec[1:2], vec[2:3] = area * x, area * y, area * z
    vec[3:4] = area
    put_columns(out_w, where, vec[...])


def pack_kernel(count, *refs):
    packed = refs[count]
    size = refs[0].shape[0]
    for at in range(count):
        packed[at * size : (at + 1) * size] = refs[at][...]


def columns_kernel(size, count, *refs):
    shards = []
    for ref in refs[:count]:
        shards += [ref.at[at : at + size] for at in range(0, ref.shape[0], size)]
    for at, shard in enumerate(shards):
        shard_features(shard, at, *refs[count:])


def put_columns(out, where, v):
    high, mid, low = parts(v)
    out[0:16, where] = jnp.concatenate([high, mid], axis=0).astype(BF16)
    out[16:32, where] = jnp.concatenate([high, low], axis=0).astype(BF16)
    out[32:48, where] = jnp.concatenate([high, mid], axis=0).astype(BF16)


def row_part(v):
    high, mid, low = parts(v)
    stacked = jnp.concatenate([high, high, mid, high, low, mid], axis=0)
    return stacked.T.astype(BF16)


def row_features(g, dirs, soft_sq, out_s, out_u, out_w, vec, small):
    piece = g.shape[1]
    each = small.shape[1]
    x, y, z = g[0:1], g[1:2], g[2:3] - 1.0
    zero = jnp.zeros((4, piece), F32)
    vec[4:8] = zero
    vec[0:1], vec[1:2], vec[2:3] = (-2.0 * turns_sq) * x, (-2.0 * turns_sq) * y, (-2.0 * turns_sq) * z
    vec[3:4] = turns_sq * (x * x + y * y + z * z + soft_sq)
    vec[4:5] = jnp.ones((1, piece), F32)
    out_s[0:piece] = row_part(vec[...])
    vec[0:1], vec[1:2], vec[2:3] = x, y, z
    vec[3:4] = jnp.ones((1, piece), F32)
    vec[4:8] = zero
    out_u[0:piece] = row_part(vec[...])
    vec[0:3] = g[3:6] * (1.0 / wavenumber)
    vec[3:4] = (x * g[3:4] + y * g[4:5] + z * g[5:6]) * (-1.0 / wavenumber)
    out_w[...] = row_part(vec[...])
    dir_x, dir_y, dir_z = dirs
    small[4:8] = jnp.zeros((4, each), F32)
    small[0:1], small[1:2], small[2:3] = (value * (-wavenumber / two_pi) for value in dirs)
    small[3:4] = dir_z * (-wavenumber / two_pi)
    out_s[piece:] = row_part(small[...])
    small[0:1], small[1:2], small[2:3] = (value * (wavenumber / tile_scale) for value in dirs)
    small[3:4] = jnp.zeros((1, each), F32)
    out_u[piece:] = row_part(small[...])


def directions(angle_ref, owner, each):
    lanes = max(each, 128)
    fit = lanes // each
    window = angle_ref[:, pl.ds(pl.multiple_of(owner // fit * lanes, lanes), lanes)]
    angles = window[:, :each]
    for k in range(1, fit):
        angles = jnp.where(lax.rem(owner, fit) == k, window[:, k * each : (k + 1) * each], angles)
    c, s = cos_sin(angles * (1.0 / two_pi))
    sin_t = s[0:1]
    return sin_t * c[1:2], sin_t * s[1:2], c[0:1]


def panel_entries(s, u, w):
    inverse = lax.rsqrt(s)
    d, x = half_tangent(s * inverse)
    d2, x2 = d * d, x * x
    q = pl.reciprocal((d2 + x2) * s)
    re = (d2 - x2) * q
    h = d * q
    im = (h + h) * x
    p = inverse * (1.0 / two_pi)
    a = p * u + w
    b = p * w - u
    return re * a - im * b, re * b + im * a


def far_entries(turn, scale):
    d, x = half_tangent(turn)
    d2, x2 = d * d, x * x
    q = scale * pl.reciprocal(d2 + x2)
    h = d * q
    return (h + h) * x, (x2 - d2) * q


def tiles_kernel(soft_sq, resume, picks, skip, *refs):
    count = len(picks)
    if resume:
        befores, refs = refs[:count], refs[count:]
        keeps, refs = refs[: 3 * count], refs[3 * count :]
        cs, cu, cw, x_ref, *refs = refs
        outs, bufs = refs[:count], refs[count:]
    else:
        geoms, refs = refs[:count], refs[count:]
        dirs_ref, cs, cu, cw, x_ref, *refs = refs
        keeps, refs = refs[: 3 * count], refs[3 * count :]
        outs, (vec, small, *bufs) = refs[:count], refs[count:]
    rows, width = keeps[0].shape[0], x_ref.shape[1]
    piece = keeps[2].shape[0]
    steps = (cs.shape[1] // CHUNK - skip) // 2
    first, second, tile_a, tile_b, acc = bufs[:3], bufs[3:6], bufs[6], bufs[7], bufs[8]

    def prepare(index):
        if not resume:
            at = 8 * picks[index]
            dirs = [dirs_ref[at + j : at + j + 1] for j in range(3)]
            row_features(geoms[index][...], dirs, soft_sq, *keeps[3 * index : 3 * index + 3], vec, small)

    def multiply(index, at, buf):
        where = pl.ds(pl.multiple_of((at + skip) * CHUNK, CHUNK), CHUNK)
        for row_ref, col_ref, hold in zip(keeps[3 * index : 3 * index + 3], (cs, cu, cw), buf):
            hold[...] = jnp.dot(row_ref[...], col_ref[:, where], preferred_element_type=F32)

    def entries(buf, tile, diagonal=None):
        for begin in range(0, rows, SUB):
            take = pl.ds(begin, SUB)
            if begin < piece:
                re, im = panel_entries(buf[0][take], buf[1][take], buf[2][take])
                if diagonal is not None:
                    down = lax.broadcasted_iota(jnp.int32, (SUB, CHUNK), 0) + begin
                    across = lax.broadcasted_iota(jnp.int32, (SUB, CHUNK), 1) + diagonal
                    re = jnp.where(down == across, 0.0, re)
                    im = jnp.where(down == across, 0.0, im)
            else:
                re, im = far_entries(buf[0][take], buf[1][take])
            tile[take, :CHUNK] = re.astype(BF16)
            tile[take, CHUNK:] = im.astype(BF16)

    def apply(index, at, tile, begin=False, end=False):
        where = pl.ds(pl.multiple_of((at + skip) * 2 * CHUNK, 2 * CHUNK), 2 * CHUNK)
        product = jnp.dot(tile[...], x_ref[where], preferred_element_type=F32)
        if not begin:
            product = acc[...] + product
        elif resume:
            product = befores[index][...] + product
        if end:
            outs[index][...] = product.astype(outs[index].dtype)
        else:
            acc[...] = product

    def two(index, step, begin, last):
        own = last and not resume and picks[index] == 0
        multiply(index, 2 * step + 1, second)
        if not begin:
            apply(index, 2 * step - 1, tile_b)
        elif index:
            apply(index - 1, 2 * steps - 1, tile_b, end=True)
        entries(first, tile_a, 0 if own and piece == 2 * CHUNK else None)
        if not last:
            multiply(index, 2 * step + 2, first)
        elif index + 1 < len(picks):
            prepare(index + 1)
            multiply(index + 1, 0, first)
        apply(index, 2 * step, tile_a, begin)
        entries(second, tile_b, piece - CHUNK if own else None)

    def body(index, step, carry):
        two(index, step, False, False)
        return carry

    prepare(0)
    multiply(0, 0, first)
    for index in range(len(picks)):
        two(index, 0, True, steps == 1)
        if steps > 1:
            lax.fori_loop(1, steps - 1, functools.partial(body, index), 0)
            two(index, steps - 1, False, True)
    apply(len(picks) - 1, 2 * steps - 1, tile_b, end=True)


def dot_first(left, right, precision=None):
    return lax.dot_general(
        left, right, (((0,), (0,)), ((), ())), precision=precision, preferred_element_type=F32
    )


def local_kernel(x_ref, g_ref, index_ref, weight_ref, blade_ref, harmonic_ref, out):
    piece, width = x_ref.shape
    half = width // 2
    count = index_ref.shape[0]
    rows = lax.axis_index("rows")
    cols = lax.axis_index("cols")
    base = (rows * lax.axis_size("cols") + cols) * piece
    ids = lax.broadcasted_iota(jnp.int32, (piece, piece), 0) + base
    m_re = jnp.zeros((piece, piece), F32)
    m_im = jnp.zeros((piece, piece), F32)
    for c in range(count):
        hit = ids == index_ref[c : c + 1]
        m_re += jnp.where(hit, weight_ref[c : c + 1], 0.0)
        m_im += jnp.where(hit, weight_ref[count + c : count + c + 1], 0.0)
    x = x_ref[...]
    first = jnp.zeros((piece, width), F32)
    second = jnp.zeros((piece, width), F32)
    for part in parts(m_re):
        first += dot_first(part.astype(BF16), x)
    for part in parts(m_im):
        second += dot_first(part.astype(BF16), x)
    g = g_ref[...]
    source = lax.broadcasted_iota(jnp.int32, (NS, 1), 0)
    src_cos, src_sin = cos_sin(source.astype(F32) * (1.0 / NS))
    dx = g[0:1] - cycle_radius * src_cos
    dy = g[1:2] - cycle_radius * src_sin
    dz = g[2:3] - cycle_height
    r_sq = dx * dx + dy * dy + dz * dz
    inverse = lax.rsqrt(r_sq)
    c, s = cos_sin(r_sq * inverse * (wavenumber / two_pi))
    g_re = c * inverse * (1.0 / four_pi)
    g_im = s * inverse * (1.0 / four_pi)
    slope = (dx * g[3:4] + dy * g[4:5] + dz * g[5:6]) * inverse
    f_re = 1.0 - slope
    f_im = slope * inverse * (-1.0 / wavenumber)
    h_re = g_re * f_re - g_im * f_im
    h_im = g_re * f_im + g_im * f_re
    turn = lax.rem(source * (blade_ref[...] * harmonic_ref[...]), NS).astype(F32) * (1.0 / NS)
    e_re, e_im = cos_sin(turn)
    lhs = jnp.concatenate([h_re, h_im], axis=0)
    rhs = jnp.concatenate(
        [jnp.concatenate([e_re, e_im], axis=1), jnp.concatenate([-e_im, e_re], axis=1)], axis=0
    )
    b = dot_first(lhs, rhs, lax.Precision.HIGHEST)
    xf = x.astype(F32)
    out[:, :half] = b[:, :half] - 0.5 * xf[:, :half] - (first[:, :half] - second[:, half:])
    out[:, half:] = b[:, half:] - 0.5 * xf[:, half:] - (first[:, half:] + second[:, :half])


def final_kernel(count, base, own, *refs):
    got, residual, far = refs[:count], refs[count], refs[count + 1]
    piece = residual.shape[0]
    total = own[...]
    for ref in got:
        total += ref[...].astype(F32)
    residual[...] = base[...] - total[:piece]
    far[...] = total[piece:]


def call(kernel, out_shape, scratch=(), name=None, cost=None, inputs=None, limit=40):
    return pl.pallas_call(
        kernel,
        out_shape=out_shape,
        scratch_shapes=list(scratch),
        compiler_params=pltpu.CompilerParams(vmem_limit_bytes=limit * 2**20),
        cost_estimate=cost,
        name=name,
        **({} if inputs is None else {"in_specs": inputs}),
    )


def TILE_COST(entries):
    return pl.CostEstimate(flops=1, bytes_accessed=2 * 10**6, transcendentals=0)


NEAR_COST = pl.CostEstimate(flops=1, bytes_accessed=2 * 10**6, transcendentals=0)


def xor_permute(value, axis, mask):
    size = lax.axis_size(axis)
    return lax.ppermute(value, axis, [(i, i ^ mask) for i in range(size)])


def local(krylov, geometry, corr_index, corr_weight, blades, harmonic, observer_angles):
    nrows = lax.axis_size("rows")
    ncols = lax.axis_size("cols")
    piece, width = krylov.shape
    soft_sq = 4.0 / (piece * nrows * ncols)
    each = observer_angles.shape[1] // (nrows * ncols)
    rows = piece + each

    masks = list(range(2, nrows, 2))
    order = [0] + masks
    payload, dirs, geometry_here = call(
        functools.partial(payload_kernel, order),
        (
            pltpu.VMEM((piece + 32, width), BF16),
            pltpu.VMEM((8 * len(order), each), F32),
            pltpu.VMEM(geometry.shape, F32),
        ),
        [pltpu.VMEM(a.shape, a.dtype) for a in (krylov, observer_angles)] + [pltpu.SemaphoreType.DMA((3,))],
        name="payload",
        inputs=[pl.BlockSpec(memory_space=pltpu.HBM)] * 3,
        limit=56,
    )(krylov, geometry, observer_angles)
    line = [payload] + [xor_permute(payload, "cols", m) for m in range(ncols - 1, 0, -1)]
    near_half, far_half = line[: ncols // 2][::-1], line[ncols // 2 :]

    plane = [geometry_here] + [xor_permute(geometry_here, "rows", m) for m in masks]

    def exchange(shards):
        packed = call(
            functools.partial(pack_kernel, len(shards)),
            jax.ShapeDtypeStruct((len(shards) * (piece + 32), width), BF16),
            name="pack",
        )(*shards)
        return xor_permute(packed, "rows", 1)

    def features(*shards):
        panels = sum(shard.shape[0] for shard in shards) // (piece + 32) * piece
        feature = jax.ShapeDtypeStruct((DEPTH, panels), BF16)
        return call(
            functools.partial(columns_kernel, piece + 32, len(shards)),
            (feature, feature, feature, jax.ShapeDtypeStruct((2 * panels, width), BF16)),
            [pltpu.VMEM((8, piece), F32)],
            name="columns",
        )(*shards)

    buf = [pltpu.VMEM((rows, CHUNK), F32)] * 2 + [pltpu.VMEM((piece, CHUNK), F32)]
    buf = buf * 2 + [pltpu.VMEM((rows, 2 * CHUNK), BF16)] * 2 + [pltpu.VMEM((rows, width), F32)]

    partial = jax.ShapeDtypeStruct((rows, width), F32)
    kept = [jax.ShapeDtypeStruct((size, DEPTH), BF16) for size in (rows, rows, piece)]
    held, keeps = {}, {}

    def tiles(picks, columns):
        found = call(
            functools.partial(tiles_kernel, soft_sq, False, picks, 0),
            (*kept * len(picks), *[partial] * len(picks)),
            [pltpu.VMEM((8, piece), F32), pltpu.VMEM((8, each), F32)] + buf,
            name="tiles",
            cost=TILE_COST(rows * columns[0].shape[1]),
        )(*[plane[pick] for pick in picks], dirs, *columns)
        for at, pick in enumerate(picks):
            keeps[pick], held[pick] = found[3 * at : 3 * at + 3], found[3 * len(picks) + at]

    def resume(picks, columns, last=False, skip=0):
        found = call(
            functools.partial(tiles_kernel, soft_sq, True, picks, skip),
            tuple(jax.ShapeDtypeStruct((rows, width), BF16 if pick and last else F32) for pick in picks),
            buf,
            name="resume",
            cost=TILE_COST(rows * columns[0].shape[1]),
        )(*[held[pick] for pick in picks], *[keep for pick in picks for keep in keeps[pick]], *columns)
        held.update(zip(picks, found))

    def after(value, *earlier):
        return lax.optimization_barrier((value, earlier))[0]

    received, dirs, early = lax.optimization_barrier((near_half[:-1], dirs, plane[1:3]))
    plane[1:3] = early
    near_half = received + near_half[-1:]
    columns = features(*near_half)
    final = len(order) - 1
    tiles(list(range(final)), columns)
    plane[final] = after(plane[final], held[0])
    tiles([final], columns)

    packed = exchange(near_half)
    far_half = after(far_half, held)
    other = exchange(far_half)
    ahead = list(range(final, final // 2, -1))
    resume(ahead, features(packed))
    other = after(other, held)
    columns = features(packed, other, *far_half)
    got = []
    groups = [ahead[i : i + 2] for i in range(0, len(ahead), 2)]
    groups += [[pick] for pick in range(final // 2, 0, -1)]
    for picks in groups:
        resume(picks, columns, True, 2 * piece * (ncols // 2) // 2 // CHUNK if picks[0] in ahead else 0)
        got += [xor_permute(held[pick], "rows", order[pick]) for pick in picks]
        coming = picks[-1] - 1
        held[coming] = after(held[coming], held[picks[-1]])
    got[:1], held[0] = lax.optimization_barrier((got[:1], held[0]))
    resume([0], columns, True)
    own = held[0]

    got[:-1], near_geometry = lax.optimization_barrier((got[:-1], after(geometry_here, own)))
    base = call(
        local_kernel,
        jax.ShapeDtypeStruct((piece, width), F32),
        name="near_and_incident",
        cost=NEAR_COST,
    )(krylov, near_geometry, corr_index, corr_weight, blades.reshape(1, -1), harmonic.reshape(1, -1))

    return call(
        functools.partial(final_kernel, len(got)),
        (jax.ShapeDtypeStruct((piece, width), F32), jax.ShapeDtypeStruct((each, width), F32)),
        name="combine",
    )(base, own, *got)


def solution(mesh):
    placed = (
        P(("rows", "cols"), None),
        P(None, ("rows", "cols")),
        P(None, ("rows", "cols")),
        P(None, ("rows", "cols")),
        P(),
        P(),
        P(),
    )
    return jax.shard_map(
        local,
        mesh=mesh,
        in_specs=placed,
        out_specs=(P(("rows", "cols"), None), P(("rows", "cols"), None)),
        check_vma=False,
    )
```

```python
import functools
import math

import jax
import jax.numpy as jnp
from jax import lax
from jax.experimental import pallas as pl
from jax.experimental.pallas import tpu as pltpu
from jax.sharding import PartitionSpec as P

NS = 64
wavenumber = 20.0
cycle_radius = 0.7
cycle_height = 1.0
four_pi = 4.0 * math.pi
two_pi = 2.0 * math.pi

COARSE_D = (-4.203673078505327, 0.9884209687656514)
COARSE_N = (-2.9883226762430346, 3.1051740325541175)
FINE_D = (-2.7704097493600783, 0.6301024476540067)
FINE_N = (0.21837236917008357, -2.1911377274692434, 1.9795254225510943)
ROUNDER = 12582912.0

turns_sq = (wavenumber / two_pi) ** 2
tile_scale = wavenumber**3 / four_pi / two_pi**2
DEPTH = 48
CHUNK = 256
SUB = 16
BF16 = jnp.bfloat16
F32 = jnp.float32


def half_tangent(turn, fine=False):
    f = turn - ((turn + ROUNDER) - ROUNDER)
    z = f * f
    if fine:
        d = (z + FINE_D[0]) * z + FINE_D[1]
        x = f * ((z * FINE_N[0] + FINE_N[1]) * z + FINE_N[2])
    else:
        d = (z + COARSE_D[0]) * z + COARSE_D[1]
        x = f * (z * COARSE_N[0] + COARSE_N[1])
    return d, x


def cos_sin(turn):
    d, x = half_tangent(turn, fine=True)
    q = 1.0 / (d * d + x * x)
    return (d * d - x * x) * q, 2.0 * d * x * q


def parts(v):
    high = v.astype(BF16).astype(F32)
    rest = v - high
    mid = rest.astype(BF16).astype(F32)
    return high, mid, rest - mid


def payload_kernel(masks, x_hbm, g_hbm, angle_hbm, out, dirs_out, vec, x_buf, angles, sem):
    piece = x_hbm.shape[0]
    each = angles.shape[1] // (lax.axis_size("rows") * lax.axis_size("cols"))
    copies = [
        pltpu.make_async_copy(src, dst, sem.at[i])
        for i, (src, dst) in enumerate(((g_hbm, vec), (angle_hbm, angles), (x_hbm, x_buf)))
    ]
    for copy in copies:
        copy.start()
    copies[0].wait()
    g = jnp.concatenate([vec[...], jnp.zeros((1, vec.shape[1]), F32)], axis=0)
    high, mid, low = parts(g)
    out[piece : piece + 16] = jnp.concatenate([high, mid], axis=0).astype(BF16)
    out[piece + 16 : piece + 32] = jnp.concatenate([low, jnp.zeros_like(low)], axis=0).astype(BF16)
    copies[1].wait()
    dirs_out[...] = jnp.zeros_like(dirs_out)
    for i, mask in enumerate(masks):
        owner = (lax.axis_index("rows") ^ mask) * lax.axis_size("cols") + lax.axis_index("cols")
        for j, value in enumerate(directions(angles, owner, each)):
            dirs_out[8 * i + j : 8 * i + j + 1] = value
    copies[2].wait()
    out[0:piece] = x_buf[...]


def shard_features(shard, at, out_s, out_u, out_w, out_x, vec):
    piece = shard.shape[0] - 32
    half = out_x.shape[1] // 2
    x = shard[0:piece]
    out_x[2 * at * piece : (2 * at + 1) * piece] = x
    turned = jnp.concatenate([-x[:, half:], x[:, :half]], axis=1)
    out_x[(2 * at + 1) * piece : (2 * at + 2) * piece] = turned
    held = shard[piece : piece + 32].astype(F32)
    g = held[0:8] + held[8:16] + held[16:24]
    where = pl.ds(at * piece, piece)
    x, y, z = g[0:1], g[1:2], g[2:3] - 1.0
    area = g[6:7] * tile_scale
    zero = jnp.zeros((4, piece), F32)
    vec[0:1], vec[1:2], vec[2:3] = x, y, z
    vec[3:4] = jnp.ones((1, piece), F32)
    vec[4:8] = zero
    vec[4:5] = turns_sq * (x * x + y * y + z * z)
    put_columns(out_s, where, vec[...])
    vec[0:3] = area * g[3:6]
    vec[3:4] = -area * (x * g[3:4] + y * g[4:5] + z * g[5:6])
    vec[4:8] = zero
    put_columns(out_u, where, vec[...])
    vec[0:1], vec[1:2], vec[2:3] = area * x, area * y, area * z
    vec[3:4] = area
    put_columns(out_w, where, vec[...])


def pack_kernel(count, *refs):
    packed = refs[count]
    size = refs[0].shape[0]
    for at in range(count):
        packed[at * size : (at + 1) * size] = refs[at][...]


def columns_kernel(size, count, *refs):
    shards = []
    for ref in refs[:count]:
        shards += [ref.at[at : at + size] for at in range(0, ref.shape[0], size)]
    for at, shard in enumerate(shards):
        shard_features(shard, at, *refs[count:])


def put_columns(out, where, v):
    high, mid, low = parts(v)
    out[0:16, where] = jnp.concatenate([high, mid], axis=0).astype(BF16)
    out[16:32, where] = jnp.concatenate([high, low], axis=0).astype(BF16)
    out[32:48, where] = jnp.concatenate([high, mid], axis=0).astype(BF16)


def row_part(v):
    high, mid, low = parts(v)
    stacked = jnp.concatenate([high, high, mid, high, low, mid], axis=0)
    return stacked.T.astype(BF16)


def row_features(g, dirs, soft_sq, out_s, out_u, out_w, vec, small):
    piece = g.shape[1]
    each = small.shape[1]
    x, y, z = g[0:1], g[1:2], g[2:3] - 1.0
    zero = jnp.zeros((4, piece), F32)
    vec[4:8] = zero
    vec[0:1], vec[1:2], vec[2:3] = (-2.0 * turns_sq) * x, (-2.0 * turns_sq) * y, (-2.0 * turns_sq) * z
    vec[3:4] = turns_sq * (x * x + y * y + z * z + soft_sq)
    vec[4:5] = jnp.ones((1, piece), F32)
    out_s[0:piece] = row_part(vec[...])
    vec[0:1], vec[1:2], vec[2:3] = x, y, z
    vec[3:4] = jnp.ones((1, piece), F32)
    vec[4:8] = zero
    out_u[0:piece] = row_part(vec[...])
    vec[0:3] = g[3:6] * (1.0 / wavenumber)
    vec[3:4] = (x * g[3:4] + y * g[4:5] + z * g[5:6]) * (-1.0 / wavenumber)
    out_w[...] = row_part(vec[...])
    dir_x, dir_y, dir_z = dirs
    small[4:8] = jnp.zeros((4, each), F32)
    small[0:1], small[1:2], small[2:3] = (value * (-wavenumber / two_pi) for value in dirs)
    small[3:4] = dir_z * (-wavenumber / two_pi)
    out_s[piece:] = row_part(small[...])
    small[0:1], small[1:2], small[2:3] = (value * (wavenumber / tile_scale) for value in dirs)
    small[3:4] = jnp.zeros((1, each), F32)
    out_u[piece:] = row_part(small[...])


def directions(angle_ref, owner, each):
    lanes = max(each, 128)
    fit = lanes // each
    window = angle_ref[:, pl.ds(pl.multiple_of(owner // fit * lanes, lanes), lanes)]
    angles = window[:, :each]
    for k in range(1, fit):
        angles = jnp.where(lax.rem(owner, fit) == k, window[:, k * each : (k + 1) * each], angles)
    c, s = cos_sin(angles * (1.0 / two_pi))
    sin_t = s[0:1]
    return sin_t * c[1:2], sin_t * s[1:2], c[0:1]


def panel_entries(s, u, w):
    inverse = lax.rsqrt(s)
    d, x = half_tangent(s * inverse)
    d2, x2 = d * d, x * x
    q = pl.reciprocal((d2 + x2) * s)
    re = (d2 - x2) * q
    h = d * q
    im = (h + h) * x
    p = inverse * (1.0 / two_pi)
    a = p * u + w
    b = p * w - u
    return re * a - im * b, re * b + im * a


def far_entries(turn, scale):
    d, x = half_tangent(turn)
    d2, x2 = d * d, x * x
    q = scale * pl.reciprocal(d2 + x2)
    h = d * q
    return (h + h) * x, (x2 - d2) * q


def tiles_kernel(soft_sq, resume, picks, skip, *refs):
    count = len(picks)
    if resume:
        befores, refs = refs[:count], refs[count:]
        keeps, refs = refs[: 3 * count], refs[3 * count :]
        cs, cu, cw, x_ref, *refs = refs
        outs, bufs = refs[:count], refs[count:]
    else:
        geoms, refs = refs[:count], refs[count:]
        dirs_ref, cs, cu, cw, x_ref, *refs = refs
        keeps, refs = refs[: 3 * count], refs[3 * count :]
        outs, (vec, small, *bufs) = refs[:count], refs[count:]
    rows, width = keeps[0].shape[0], x_ref.shape[1]
    piece = keeps[2].shape[0]
    steps = (cs.shape[1] // CHUNK - skip) // 2
    first, second, tile_a, tile_b, acc = bufs[:3], bufs[3:6], bufs[6], bufs[7], bufs[8]

    def prepare(index):
        if not resume:
            at = 8 * picks[index]
            dirs = [dirs_ref[at + j : at + j + 1] for j in range(3)]
            row_features(geoms[index][...], dirs, soft_sq, *keeps[3 * index : 3 * index + 3], vec, small)

    def multiply(index, at, buf):
        where = pl.ds(pl.multiple_of((at + skip) * CHUNK, CHUNK), CHUNK)
        for row_ref, col_ref, hold in zip(keeps[3 * index : 3 * index + 3], (cs, cu, cw), buf):
            hold[...] = jnp.dot(row_ref[...], col_ref[:, where], preferred_element_type=F32)

    def entries(buf, tile, diagonal=None):
        for begin in range(0, rows, SUB):
            take = pl.ds(begin, SUB)
            if begin < piece:
                re, im = panel_entries(buf[0][take], buf[1][take], buf[2][take])
                if diagonal is not None:
                    down = lax.broadcasted_iota(jnp.int32, (SUB, CHUNK), 0) + begin
                    across = lax.broadcasted_iota(jnp.int32, (SUB, CHUNK), 1) + diagonal
                    re = jnp.where(down == across, 0.0, re)
                    im = jnp.where(down == across, 0.0, im)
            else:
                re, im = far_entries(buf[0][take], buf[1][take])
            tile[take, :CHUNK] = re.astype(BF16)
            tile[take, CHUNK:] = im.astype(BF16)

    def apply(index, at, tile, begin=False, end=False):
        where = pl.ds(pl.multiple_of((at + skip) * 2 * CHUNK, 2 * CHUNK), 2 * CHUNK)
        product = jnp.dot(tile[...], x_ref[where], preferred_element_type=F32)
        if not begin:
            product = acc[...] + product
        elif resume:
            product = befores[index][...] + product
        if end:
            outs[index][...] = product.astype(outs[index].dtype)
        else:
            acc[...] = product

    def two(index, step, begin, last):
        own = last and not resume and picks[index] == 0
        multiply(index, 2 * step + 1, second)
        if not begin:
            apply(index, 2 * step - 1, tile_b)
        elif index:
            apply(index - 1, 2 * steps - 1, tile_b, end=True)
        entries(first, tile_a, 0 if own and piece == 2 * CHUNK else None)
        if not last:
            multiply(index, 2 * step + 2, first)
        elif index + 1 < len(picks):
            prepare(index + 1)
            multiply(index + 1, 0, first)
        apply(index, 2 * step, tile_a, begin)
        entries(second, tile_b, piece - CHUNK if own else None)

    def body(index, step, carry):
        two(index, step, False, False)
        return carry

    prepare(0)
    multiply(0, 0, first)
    for index in range(len(picks)):
        two(index, 0, True, steps == 1)
        if steps > 1:
            lax.fori_loop(1, steps - 1, functools.partial(body, index), 0)
            two(index, steps - 1, False, True)
    apply(len(picks) - 1, 2 * steps - 1, tile_b, end=True)


def dot_first(left, right, precision=None):
    return lax.dot_general(
        left, right, (((0,), (0,)), ((), ())), precision=precision, preferred_element_type=F32
    )


def local_kernel(x_ref, g_ref, index_ref, weight_ref, blade_ref, harmonic_ref, out):
    piece, width = x_ref.shape
    half = width // 2
    count = index_ref.shape[0]
    rows = lax.axis_index("rows")
    cols = lax.axis_index("cols")
    base = (rows * lax.axis_size("cols") + cols) * piece
    ids = lax.broadcasted_iota(jnp.int32, (piece, piece), 0) + base
    m_re = jnp.zeros((piece, piece), F32)
    m_im = jnp.zeros((piece, piece), F32)
    for c in range(count):
        hit = ids == index_ref[c : c + 1]
        m_re += jnp.where(hit, weight_ref[c : c + 1], 0.0)
        m_im += jnp.where(hit, weight_ref[count + c : count + c + 1], 0.0)
    x = x_ref[...]
    first = jnp.zeros((piece, width), F32)
    second = jnp.zeros((piece, width), F32)
    for part in parts(m_re):
        first += dot_first(part.astype(BF16), x)
    for part in parts(m_im):
        second += dot_first(part.astype(BF16), x)
    g = g_ref[...]
    source = lax.broadcasted_iota(jnp.int32, (NS, 1), 0)
    src_cos, src_sin = cos_sin(source.astype(F32) * (1.0 / NS))
    dx = g[0:1] - cycle_radius * src_cos
    dy = g[1:2] - cycle_radius * src_sin
    dz = g[2:3] - cycle_height
    r_sq = dx * dx + dy * dy + dz * dz
    inverse = lax.rsqrt(r_sq)
    c, s = cos_sin(r_sq * inverse * (wavenumber / two_pi))
    g_re = c * inverse * (1.0 / four_pi)
    g_im = s * inverse * (1.0 / four_pi)
    slope = (dx * g[3:4] + dy * g[4:5] + dz * g[5:6]) * inverse
    f_re = 1.0 - slope
    f_im = slope * inverse * (-1.0 / wavenumber)
    h_re = g_re * f_re - g_im * f_im
    h_im = g_re * f_im + g_im * f_re
    turn = lax.rem(source * (blade_ref[...] * harmonic_ref[...]), NS).astype(F32) * (1.0 / NS)
    e_re, e_im = cos_sin(turn)
    lhs = jnp.concatenate([h_re, h_im], axis=0)
    rhs = jnp.concatenate(
        [jnp.concatenate([e_re, e_im], axis=1), jnp.concatenate([-e_im, e_re], axis=1)], axis=0
    )
    b = dot_first(lhs, rhs, lax.Precision.HIGHEST)
    xf = x.astype(F32)
    out[:, :half] = b[:, :half] - 0.5 * xf[:, :half] - (first[:, :half] - second[:, half:])
    out[:, half:] = b[:, half:] - 0.5 * xf[:, half:] - (first[:, half:] + second[:, :half])


def collect_kernel(count, base, own, *refs):
    got, out = refs[:count], refs[count]
    piece = base.shape[0]
    total = own[...]
    for ref in got:
        total += ref[...].astype(F32)
    out[:piece] = base[...] - total[:piece]
    out[piece:] = total[piece:]


def final_kernel(most, got, residual, far):
    piece = residual.shape[0]
    residual[...] = most[:piece] - got[:piece].astype(F32)
    far[...] = most[piece:] + got[piece:].astype(F32)


def call(kernel, out_shape, scratch=(), name=None, cost=None, inputs=None, limit=40):
    return pl.pallas_call(
        kernel,
        out_shape=out_shape,
        scratch_shapes=list(scratch),
        compiler_params=pltpu.CompilerParams(vmem_limit_bytes=limit * 2**20),
        cost_estimate=cost,
        name=name,
        **({} if inputs is None else {"in_specs": inputs}),
    )


def TILE_COST(entries):
    return pl.CostEstimate(flops=1, bytes_accessed=2 * 10**6, transcendentals=0)


NEAR_COST = pl.CostEstimate(flops=1, bytes_accessed=2 * 10**6, transcendentals=0)


def xor_permute(value, axis, mask):
    size = lax.axis_size(axis)
    return lax.ppermute(value, axis, [(i, i ^ mask) for i in range(size)])


def local(krylov, geometry, corr_index, corr_weight, blades, harmonic, observer_angles):
    nrows = lax.axis_size("rows")
    ncols = lax.axis_size("cols")
    piece, width = krylov.shape
    soft_sq = 4.0 / (piece * nrows * ncols)
    each = observer_angles.shape[1] // (nrows * ncols)
    rows = piece + each

    masks = list(range(2, nrows, 2))
    order = [0] + masks
    payload, dirs, geometry_here = call(
        functools.partial(payload_kernel, order),
        (
            pltpu.VMEM((piece + 32, width), BF16),
            pltpu.VMEM((8 * len(order), each), F32),
            pltpu.VMEM(geometry.shape, F32),
        ),
        [pltpu.VMEM(a.shape, a.dtype) for a in (krylov, observer_angles)] + [pltpu.SemaphoreType.DMA((3,))],
        name="payload",
        inputs=[pl.BlockSpec(memory_space=pltpu.HBM)] * 3,
        limit=56,
    )(krylov, geometry, observer_angles)
    line = [payload] + [xor_permute(payload, "cols", m) for m in range(ncols - 1, 0, -1)]
    near_half, far_half = line[: ncols // 2][::-1], line[ncols // 2 :]

    plane = [geometry_here] + [xor_permute(geometry_here, "rows", m) for m in masks]

    def exchange(shards):
        packed = call(
            functools.partial(pack_kernel, len(shards)),
            jax.ShapeDtypeStruct((len(shards) * (piece + 32), width), BF16),
            name="pack",
        )(*shards)
        return xor_permute(packed, "rows", 1)

    def features(*shards):
        panels = sum(shard.shape[0] for shard in shards) // (piece + 32) * piece
        feature = jax.ShapeDtypeStruct((DEPTH, panels), BF16)
        return call(
            functools.partial(columns_kernel, piece + 32, len(shards)),
            (feature, feature, feature, jax.ShapeDtypeStruct((2 * panels, width), BF16)),
            [pltpu.VMEM((8, piece), F32)],
            name="columns",
        )(*shards)

    buf = [pltpu.VMEM((rows, CHUNK), F32)] * 2 + [pltpu.VMEM((piece, CHUNK), F32)]
    buf = buf * 2 + [pltpu.VMEM((rows, 2 * CHUNK), BF16)] * 2 + [pltpu.VMEM((rows, width), F32)]

    partial = jax.ShapeDtypeStruct((rows, width), F32)
    kept = [jax.ShapeDtypeStruct((size, DEPTH), BF16) for size in (rows, rows, piece)]
    held, keeps = {}, {}

    def tiles(picks, columns):
        found = call(
            functools.partial(tiles_kernel, soft_sq, False, picks, 0),
            (*kept * len(picks), *[partial] * len(picks)),
            [pltpu.VMEM((8, piece), F32), pltpu.VMEM((8, each), F32)] + buf,
            name="tiles",
            cost=TILE_COST(rows * columns[0].shape[1]),
        )(*[plane[pick] for pick in picks], dirs, *columns)
        for at, pick in enumerate(picks):
            keeps[pick], held[pick] = found[3 * at : 3 * at + 3], found[3 * len(picks) + at]

    def resume(picks, columns, last=False, skip=0):
        found = call(
            functools.partial(tiles_kernel, soft_sq, True, picks, skip),
            tuple(jax.ShapeDtypeStruct((rows, width), BF16 if pick and last else F32) for pick in picks),
            buf,
            name="resume",
            cost=TILE_COST(rows * columns[0].shape[1]),
        )(*[held[pick] for pick in picks], *[keep for pick in picks for keep in keeps[pick]], *columns)
        held.update(zip(picks, found))

    def after(value, *earlier):
        return lax.optimization_barrier((value, earlier))[0]

    received, dirs, early = lax.optimization_barrier((near_half[:-1], dirs, plane[1:3]))
    plane[1:3] = early
    near_half = received + near_half[-1:]
    columns = features(*near_half)
    final = len(order) - 1
    tiles(list(range(final)), columns)
    plane[final] = after(plane[final], held[0])
    tiles([final], columns)

    packed = exchange(near_half)
    far_half = after(far_half, held)
    other = exchange(far_half)
    ahead = list(range(final, final // 2, -1))
    resume(ahead, features(packed))
    other = after(other, held)
    columns = features(packed, other, *far_half)
    got = []
    groups = [ahead[i : i + 2] for i in range(0, len(ahead), 2)]
    groups += [[pick] for pick in range(final // 2, 0, -1)]
    for picks in groups:
        resume(picks, columns, True, 2 * piece * (ncols // 2) // 2 // CHUNK if picks[0] in ahead else 0)
        got += [xor_permute(held[pick], "rows", order[pick]) for pick in picks]
        coming = picks[-1] - 1
        held[coming] = after(held[coming], held[picks[-1]])

    base = call(
        local_kernel,
        jax.ShapeDtypeStruct((piece, width), F32),
        name="near_and_incident",
        cost=NEAR_COST,
    )(krylov, after(geometry_here, held[1]), corr_index, corr_weight, blades.reshape(1, -1), harmonic.reshape(1, -1))
    got[:1], held[0] = lax.optimization_barrier((got[:1], after(held[0], base)))
    resume([0], columns, True)
    most = call(
        functools.partial(collect_kernel, len(got) - 1),
        jax.ShapeDtypeStruct((rows, width), F32),
        name="collect",
        cost=NEAR_COST,
    )(base, held[0], *got[:-1])

    return call(
        final_kernel,
        (jax.ShapeDtypeStruct((piece, width), F32), jax.ShapeDtypeStruct((each, width), F32)),
        name="combine",
    )(most, got[-1])


def solution(mesh):
    placed = (
        P(("rows", "cols"), None),
        P(None, ("rows", "cols")),
        P(None, ("rows", "cols")),
        P(None, ("rows", "cols")),
        P(),
        P(),
        P(),
    )
    return jax.shard_map(
        local,
        mesh=mesh,
        in_specs=placed,
        out_specs=(P(("rows", "cols"), None), P(("rows", "cols"), None)),
        check_vma=False,
    )
```
